32 devices in a mesh: row: 4 (over x, core), col: 8 (over z, y).
Axes of the slice: x: 2, y: 2, z: 4, core: 2. Of those that a mesh axis runs over, the one named last changes fastest.
Arguments:
- inputs: bfloat16 [256, 8192], P(None, 'row'), may hold values from -6 to 6
- gate_weight: bfloat16 [8192, 28672], P('row', 'col'), may hold values from -0.0625 to 0.0625
- up_weight: bfloat16 [8192, 28672], P('row', 'col'), may hold values from -0.0625 to 0.0625
- hidden_grad: bfloat16 [256, 28672], P('row', 'col'), may hold values from -6 to 6
Outputs:
- hidden: bfloat16 [256, 28672], P('row', 'col')
- input_grad: bfloat16 [256, 8192], P('col', 'row')
- gate_weight_grad: bfloat16 [8192, 28672], P('row', 'col')
- up_weight_grad: bfloat16 [8192, 28672], P('row', 'col')
The draws below stay inside these ranges and needn't reach their ends.
All inputs are finite; a program needn't handle non-finite values.
Results may differ from the reference program's by a relative error of at most 0.005.
Values may be sent and summed in bfloat16 or wider, within the bound.
No kernel may reach another device: no remote copies, remote signals or barrier semaphores. Data moves between devices by JAX's collectives and lax.ppermute only.
A program may use at most 192 MiB of HBM per device.

```python
import jax
import jax.numpy as jnp

D = 8192
FF = 28672
TOKENS = 256


def raised(result, rng, source, target, blocks, factor):
    owner, partner = [(jnp.arange(result.shape[position]) // (result.shape[position] // blocks)).reshape([-1 if axis == position else 1 for axis in range(result.ndim)]) for position in (source, target)]
    chosen = jax.random.permutation(rng, blocks)[partner]
    strong = (owner == chosen) | (owner == (partner + blocks // 2) % blocks)
    return jnp.where(strong, factor * result, result)


def block_scale(own_key, dims, pieces, low, largest):
    factor_of, own = 1.0, jax.random.fold_in(own_key, 6)
    for position, parts in pieces:
        draws = jnp.exp(jax.random.uniform(jax.random.fold_in(own, position), (parts,), jnp.float32, low / len(pieces), largest / len(pieces)))
        factor_of = factor_of * jnp.repeat(draws, dims[position] // parts).reshape([-1 if axis == position else 1 for axis in range(len(dims))])
    return factor_of


def normal_values(stream_key, dims, scale, limit, pieces=(), held_as=jnp.bfloat16):
    values = scale * jax.random.normal(stream_key, dims, jnp.float32)
    if pieces:
        values = values * block_scale(stream_key, dims, pieces, -0.22, 0.18)
    return jnp.clip(values, -limit, limit).astype(held_as)


def noise_with(own_key, extent, spread, reach, pieces, heavy, held_as=jnp.bfloat16):
    array = spread * jax.random.normal(own_key, extent, jnp.float32)
    if pieces:
        array = array * block_scale(own_key, extent, pieces, -0.22, 0.18)
    return jnp.clip(raised(array, jax.random.fold_in(own_key, 3), *heavy), -reach, reach).astype(held_as)


def setup_inputs(seed: int = 0) -> dict:
    key_of = jax.random.split(jax.random.key(seed), 5)
    return {
        "inputs": noise_with(key_of[0], (TOKENS, D), 1.0, 6.0, ((1, 4),), (1, 0, 4, 2.0)),
        "gate_weight": normal_values(key_of[1], (D, FF), D ** -0.5, 0.0625, ((0, 4), (1, 8))),
        "up_weight": normal_values(key_of[2], (D, FF), D ** -0.5, 0.0625, ((0, 4), (1, 8))),
        "hidden_grad": noise_with(key_of[3], (TOKENS, FF), 1.0, 6.0, ((0, 4), (1, 8)), (1, 0, 8, 2.0)),
    }


def reference(inputs, gate_weight, up_weight, hidden_grad):
    gate_pre = jnp.dot(inputs, gate_weight, preferred_element_type=jnp.float32)
    up_pre = jnp.dot(inputs, up_weight, preferred_element_type=jnp.float32)
    sigma_gate = jax.nn.sigmoid(gate_pre)
    hidden = (gate_pre * sigma_gate * up_pre).astype(jnp.bfloat16)
    upstream = hidden_grad.astype(jnp.float32)
    gate_grad = (upstream * up_pre * sigma_gate * (1.0 + gate_pre * (1.0 - sigma_gate))).astype(jnp.bfloat16)
    up_grad = (upstream * gate_pre * sigma_gate).astype(jnp.bfloat16)
    input_grad = (jnp.dot(gate_grad, gate_weight.T, preferred_element_type=jnp.float32)
                  + jnp.dot(up_grad, up_weight.T, preferred_element_type=jnp.float32)).astype(jnp.bfloat16)
    gate_weight_grad = jnp.dot(inputs.T, gate_grad, preferred_element_type=jnp.float32).astype(jnp.bfloat16)
    up_weight_grad = jnp.dot(inputs.T, up_grad, preferred_element_type=jnp.float32).astype(jnp.bfloat16)
    return hidden, input_grad, gate_weight_grad, up_weight_grad
```

```python
import functools

import jax
import jax.numpy as jnp
from jax import lax
from jax.experimental import pallas as pl
from jax.experimental.pallas import tpu as pltpu
from jax.sharding import PartitionSpec as P

BF16 = jnp.bfloat16
F32 = jnp.float32
VMEM_BYTES = 40 * 1024 * 1024
SHARES = (2, 4, 4, 4)


def chunk_list(width):
    block = 256 if width % 256 == 0 else 128
    units = width // block
    total = sum(SHARES)
    edges = [0]
    run = 0
    for share in SHARES:
        run += share
        edges.append(max(min(units, round(units * run / total)), edges[-1]))
    return block, [(a, b - a) for a, b in zip(edges, edges[1:]) if b > a]


def forward_kernel(quarters, rows, x_ref, gate_ref, up_ref, keep_ref, send_ref, total):
    me = lax.axis_index("row")
    x = x_ref[...]
    for k, w_ref in enumerate((gate_ref, up_ref)):
        total[k] = jnp.dot(x, w_ref[...], preferred_element_type=F32)
    outer, core = me // 2, me % 2
    for step in range(quarters // 2):
        there = (outer + step) % (quarters // 2) * 2
        mine = pl.multiple_of((there + core) * rows, rows)
        other = pl.multiple_of((there + 1 - core) * rows, rows)
        for k in range(2):
            keep_ref[k, step] = total[k, pl.ds(mine, rows), :]
            send_ref[k, step] = total[k, pl.ds(other, rows), :].astype(BF16)


def forward_part(quarters, block, start, count, x, gate_weight, up_weight):
    tokens, depth = x.shape
    rows = tokens // quarters
    outer = quarters // 2
    weight = pl.BlockSpec((depth, block), lambda j: (0, start + j))
    out = pl.BlockSpec((2, outer, rows, block), lambda j: (0, 0, 0, j))
    shape = (2, outer, rows, count * block)
    return pl.pallas_call(
        functools.partial(forward_kernel, quarters, rows),
        grid=(count,),
        in_specs=[pl.BlockSpec((tokens, depth), lambda j: (0, 0)), weight, weight],
        out_specs=[out, out],
        out_shape=[jax.ShapeDtypeStruct(shape, F32), jax.ShapeDtypeStruct(shape, BF16)],
        scratch_shapes=[pltpu.VMEM((2, tokens, block), F32)],
        compiler_params=pltpu.CompilerParams(vmem_limit_bytes=VMEM_BYTES),
        cost_estimate=pl.CostEstimate(
            flops=4 * tokens * depth * count * block,
            bytes_accessed=4 * depth * count * block,
            transcendentals=0,
        ),
        name="forward_part",
    )(x, gate_weight, up_weight)


def backward_kernel(quarters, rows, first, *refs):
    xt_ref, gate_ref, up_ref = refs[:3]
    pieces = refs[3 : 3 + quarters]
    rest = refs[3 + quarters :]
    acc_in = None
    if not first:
        acc_in, rest = rest[0], rest[3:]
    gate_out, up_out, acc_ref, grads = rest
    me = lax.axis_index("row")
    outer, core = me // 2, me % 2
    for j, piece in enumerate(pieces):
        step, swap = j // 2, j % 2
        there = (outer + quarters // 2 - step) % (quarters // 2) * 2
        at = pl.multiple_of((there + (core + swap) % 2) * rows, rows)
        for k in range(2):
            grads[k, pl.ds(at, rows), :] = piece[k]
    xt = xt_ref[...]
    gate_out[...] = jnp.dot(xt, grads[0], preferred_element_type=F32).astype(BF16)
    up_out[...] = jnp.dot(xt, grads[1], preferred_element_type=F32).astype(BF16)
    dims = (((1,), (1,)), ((), ()))
    term = lax.dot_general(grads[0], gate_ref[...], dims, preferred_element_type=F32)
    term += lax.dot_general(grads[1], up_ref[...], dims, preferred_element_type=F32)

    @pl.when(pl.program_id(0) == 0)
    def _():
        acc_ref[...] = term if first else acc_in[...] + term

    @pl.when(pl.program_id(0) > 0)
    def _():
        acc_ref[...] += term


def backward_part(quarters, block, start, count, xt, gate_weight, up_weight, pieces, state):
    depth, tokens = xt.shape
    width = gate_weight.shape[1]
    rows = tokens // quarters
    weight = pl.BlockSpec((depth, block), lambda j: (0, start + j))
    acc = pl.BlockSpec((tokens, depth), lambda j: (0, 0))
    piece = pl.BlockSpec((2, rows, block), lambda j: (0, 0, j))
    in_specs = [pl.BlockSpec((depth, tokens), lambda j: (0, 0)), weight, weight]
    in_specs += [piece] * quarters
    first = state is None
    args = [xt, gate_weight, up_weight, *pieces]
    aliases = {}
    if not first:
        aliases = {len(args): 2, len(args) + 1: 0, len(args) + 2: 1}
        args += [state[2], state[0], state[1]]
        in_specs += [acc, pl.BlockSpec(memory_space=pl.ANY), pl.BlockSpec(memory_space=pl.ANY)]
    grad = jax.ShapeDtypeStruct((depth, width), BF16)
    return pl.pallas_call(
        functools.partial(backward_kernel, quarters, rows, first),
        grid=(count,),
        in_specs=in_specs,
        out_specs=[weight, weight, acc],
        out_shape=[grad, grad, jax.ShapeDtypeStruct((tokens, depth), F32)],
        scratch_shapes=[pltpu.VMEM((2, tokens, block), BF16)],
        input_output_aliases=aliases,
        compiler_params=pltpu.CompilerParams(vmem_limit_bytes=VMEM_BYTES),
        cost_estimate=pl.CostEstimate(
            flops=8 * tokens * depth * count * block,
            bytes_accessed=8 * depth * count * block,
            transcendentals=0,
        ),
        name="backward_part",
    )(*args)


def local(quarters, columns, inputs, gate_weight, up_weight, hidden_grad):
    outer = quarters // 2
    block, chunks = chunk_list(gate_weight.shape[1])
    swap = [(r, r ^ 1) for r in range(quarters)]

    def sibling(value):
        return lax.ppermute(value, "row", swap)

    def across(value, step):
        moves = [(r, (r // 2 + step) % outer * 2 + r % 2) for r in range(quarters)]
        return lax.ppermute(value, "row", moves)

    parts = [
        forward_part(quarters, block, start, count, inputs, gate_weight, up_weight)
        for start, count in chunks
    ]
    xt = inputs.T
    hidden_parts = []
    grad_parts = []
    for (start, count), (keep, send) in zip(chunks, parts):
        both = keep + sibling(send).astype(F32)
        pre = both[:, 0]
        for step in range(1, outer):
            pre = pre + across(both[:, step].astype(BF16), step).astype(F32)
        gate_pre, up_pre = pre[0], pre[1]
        sigma_gate = jax.nn.sigmoid(gate_pre)
        hidden_parts.append((gate_pre * sigma_gate * up_pre).astype(BF16))
        upstream = hidden_grad[:, start * block : (start + count) * block].astype(F32)
        gate_grad = upstream * up_pre * sigma_gate * (1.0 + gate_pre * (1.0 - sigma_gate))
        up_grad = upstream * gate_pre * sigma_gate
        mine = jnp.stack([gate_grad.astype(BF16), up_grad.astype(BF16)])
        pieces = [mine, sibling(mine)]
        for step in range(1, outer):
            far = across(mine, step)
            pieces += [far, sibling(far)]
        grad_parts.append(pieces)

    state = None
    for (start, count), pieces in zip(chunks, grad_parts):
        state = backward_part(
            quarters, block, start, count, xt, gate_weight, up_weight, pieces, state
        )
    gate_total, up_total, total = state

    rows = total.shape[0] // columns
    total = total.reshape(columns, rows, total.shape[1])
    position = lax.axis_index("col")
    bit = 1
    while bit < columns:
        mine = (position // bit) % 2
        pairs = total.reshape(total.shape[0] // 2, 2, rows, total.shape[2])
        keep = lax.dynamic_index_in_dim(pairs, mine, 1, keepdims=False)
        send = lax.dynamic_index_in_dim(pairs, 1 - mine, 1, keepdims=False)
        moves = [(c, c ^ bit) for c in range(columns)]
        total = keep + lax.ppermute(send.astype(BF16), "col", moves).astype(F32)
        bit *= 2
    input_grad = total[0].astype(BF16)
    return jnp.concatenate(hidden_parts, axis=1), input_grad, gate_total, up_total


def solution(mesh):
    return jax.shard_map(
        functools.partial(local, mesh.shape["row"], mesh.shape["col"]),
        mesh=mesh,
        in_specs=(P(None, "row"), P("row", "col"), P("row", "col"), P("row", "col")),
        out_specs=(P("row", "col"), P("col", "row"), P("row", "col"), P("row", "col")),
        check_vma=False,
    )
```

```python
import functools

import jax
import jax.numpy as jnp
from jax import lax
from jax.experimental import pallas as pl
from jax.experimental.pallas import tpu as pltpu
from jax.sharding import PartitionSpec as P

BF16 = jnp.bfloat16
F32 = jnp.float32
VMEM_BYTES = 44 * 1024 * 1024
SHARES = (2, 4, 4, 4)
WHOLE = pl.BlockSpec(memory_space=pltpu.VMEM)
REMOTE = pl.BlockSpec(memory_space=pl.ANY)


def chunk_list(width):
    block = 256 if width % 256 == 0 else 128
    units = width // block
    total = sum(SHARES)
    edges = [0]
    run = 0
    for share in SHARES:
        run += share
        edges.append(max(min(units, round(units * run / total)), edges[-1]))
    return block, [(a, b - a) for a, b in zip(edges, edges[1:]) if b > a]


def call(kernel, name, in_specs, out_specs, out_shape, scratch, flops, moved, args, aliases=None):
    return pl.pallas_call(
        kernel,
        in_specs=in_specs,
        out_specs=out_specs,
        out_shape=out_shape,
        scratch_shapes=scratch,
        input_output_aliases=aliases or {},
        compiler_params=pltpu.CompilerParams(vmem_limit_bytes=VMEM_BYTES),
        cost_estimate=pl.CostEstimate(flops=flops, bytes_accessed=moved, transcendentals=0),
        name=name,
    )(*args)


def forward_kernel(quarters, rows, block, start, count, waits_for, x_ref, gate_ref, up_ref, *refs):
    own_ref, far_ref, send_ref, weights, total, sems = refs[waits_for:]
    copies = []
    for j in range(count):
        columns = pl.ds((start + j) * block, block)
        pair = [
            pltpu.make_async_copy(ref.at[:, columns], weights.at[k, j], sems.at[k, j])
            for k, ref in enumerate((gate_ref, up_ref))
        ]
        for copy in pair:
            copy.start()
        copies.append(pair)
    outer = quarters // 2
    me = lax.axis_index("row")
    place, core = me // 2, me % 2
    x = x_ref[...]
    for j in range(count):
        at = slice(j * block, (j + 1) * block)
        for k in range(2):
            copies[j][k].wait()
            total[k] = jnp.dot(x, weights[k, j], preferred_element_type=F32)
        for step in range(outer):
            there = (place + step) % outer * 2
            mine = pl.multiple_of((there + core) * rows, rows)
            other = pl.multiple_of((there + 1 - core) * rows, rows)
            for k in range(2):
                kept = total[k, pl.ds(mine, rows), :]
                if step == 0:
                    own_ref[k, :, at] = kept
                else:
                    far_ref[step - 1, k, :, at] = kept
                send_ref[step, k, :, at] = total[k, pl.ds(other, rows), :].astype(BF16)


def forward_part(quarters, block, start, count, x, gate_weight, up_weight, after):
    tokens, depth = x.shape
    rows = tokens // quarters
    outer = quarters // 2
    width = count * block
    return call(
        functools.partial(forward_kernel, quarters, rows, block, start, count, len(after)),
        "forward_part",
        [WHOLE, REMOTE, REMOTE] + [REMOTE] * len(after),
        [WHOLE] * 3,
        [
            jax.ShapeDtypeStruct((2, rows, width), F32),
            jax.ShapeDtypeStruct((outer - 1, 2, rows, width), F32),
            jax.ShapeDtypeStruct((outer, 2, rows, width), BF16),
        ],
        [
            pltpu.VMEM((2, count, depth, block), BF16),
            pltpu.VMEM((2, tokens, block), F32),
            pltpu.SemaphoreType.DMA((2, count)),
        ],
        4 * tokens * depth * width,
        4 * depth * width,
        (x, gate_weight, up_weight, *after),
    )


def middle_kernel(outer, at, first, own_ref, got_ref, upstream_ref, *refs):
    far_refs, rest = refs[: outer - 1], refs[outer - 1 :]
    if not first:
        rest[1][...] = rest[0][...]
        rest = rest[1:]
    hidden_ref, grads_ref = rest
    gate_pre = own_ref[0] + got_ref[0, 0].astype(F32)
    up_pre = own_ref[1] + got_ref[0, 1].astype(F32)
    for far in far_refs:
        gate_pre += far[0].astype(F32)
        up_pre += far[1].astype(F32)
    sigma_gate = jax.nn.sigmoid(gate_pre)
    upstream = upstream_ref[:, at].astype(F32)
    gated = gate_pre * sigma_gate
    hidden_ref[:, at] = (gated * up_pre).astype(BF16)
    slope = sigma_gate * (1.0 + gate_pre * (1.0 - sigma_gate))
    grads_ref[0] = (upstream * up_pre * slope).astype(BF16)
    grads_ref[1] = (upstream * gated).astype(BF16)


def middle_part(outer, at, own, got, far, hidden_grad, hidden):
    rows, width = own.shape[1:]
    first = hidden is None
    args = [own, got, hidden_grad, *far] + ([] if first else [hidden])
    return call(
        functools.partial(middle_kernel, outer, at, first),
        "middle_part",
        [WHOLE] * len(args),
        [WHOLE] * 2,
        [
            jax.ShapeDtypeStruct(hidden_grad.shape, BF16),
            jax.ShapeDtypeStruct((2, rows, width), BF16),
        ],
        [],
        20 * rows * width,
        8 * rows * width,
        args,
    )


def input_kernel(quarters, rows, split, columns, first, gate_ref, up_ref, *refs):
    pieces, rest = refs[:quarters], refs[quarters:]
    if not first:
        earlier, rest = rest[:2], rest[2:]
    halves, (grads, weights, sems) = rest[:2], rest[2:]
    parts, deep = split
    copies = []
    for d in range(parts):
        pair = [
            pltpu.make_async_copy(
                ref.at[pl.ds(d * deep, deep), columns], weights.at[k, d], sems.at[k, d]
            )
            for k, ref in enumerate((gate_ref, up_ref))
        ]
        for copy in pair:
            copy.start()
        copies.append(pair)
    outer = quarters // 2
    me = lax.axis_index("row")
    place, core = me // 2, me % 2
    for j, piece in enumerate(pieces):
        step, swap = j // 2, j % 2
        there = (place + outer - step) % outer * 2
        at = pl.multiple_of((there + (core + swap) % 2) * rows, rows)
        for k in range(2):
            grads[k, pl.ds(at, rows), :] = piece[k]
    dims = (((1,), (1,)), ((), ()))
    for d in range(parts):
        half, at = d // (parts // 2), pl.ds(d % (parts // 2) * deep, deep)
        copies[d][0].wait()
        term = lax.dot_general(grads[0], weights[0, d], dims, preferred_element_type=F32)
        copies[d][1].wait()
        term += lax.dot_general(grads[1], weights[1, d], dims, preferred_element_type=F32)
        halves[half][:, at] = term if first else earlier[half][:, at] + term


def input_part(quarters, block, start, count, gate_weight, up_weight, pieces, acc):
    depth = gate_weight.shape[0]
    rows = pieces[0].shape[1]
    tokens = rows * quarters
    width = count * block
    deep = 256 if depth % 256 == 0 else 128
    split = (depth // deep, deep)
    first = acc is None
    args = [gate_weight, up_weight, *pieces] + ([] if first else acc)
    half = jax.ShapeDtypeStruct((tokens, depth // 2), F32)
    *acc, grads = call(
        functools.partial(
            input_kernel, quarters, rows, split, pl.ds(start * block, width), first
        ),
        "input_part",
        [REMOTE] * 2 + [WHOLE] * (len(args) - 2),
        [WHOLE] * 3,
        [half, half, jax.ShapeDtypeStruct((2, tokens, width), BF16)],
        [
            pltpu.VMEM((2, split[0], deep, width), BF16),
            pltpu.SemaphoreType.DMA((2, split[0])),
        ],
        4 * tokens * depth * width,
        4 * depth * width,
        args,
    )
    return acc, grads


def weight_kernel(block, start, count, skipped, xt_ref, grads_ref, *refs):
    gate_out, up_out, products, sems = refs[skipped:]
    xt = xt_ref[...]
    copies = []
    for j in range(count):
        for k, out in enumerate((gate_out, up_out)):
            piece = grads_ref[k, :, j * block : (j + 1) * block]
            products[k, j] = jnp.dot(xt, piece, preferred_element_type=F32).astype(BF16)
            copy = pltpu.make_async_copy(
                products.at[k, j], out.at[:, pl.ds((start + j) * block, block)], sems.at[k, j]
            )
            copy.start()
            copies.append(copy)
    for copy in copies:
        copy.wait()


def weight_part(block, start, count, full, xt, grads, state, after):
    depth, tokens = xt.shape
    width = count * block
    args = [xt, grads, *after, *state]
    first = 2 + len(after)
    aliases = {first + k: k for k in range(len(state))}
    grad = jax.ShapeDtypeStruct((depth, full), BF16)
    return call(
        functools.partial(weight_kernel, block, start, count, len(args) - 2),
        "weight_part",
        [WHOLE] * 2 + [REMOTE] * len(after) + [REMOTE] * len(state),
        [REMOTE] * 2,
        [grad, grad],
        [
            pltpu.VMEM((2, count, depth, block), BF16),
            pltpu.SemaphoreType.DMA((2, count)),
        ],
        4 * tokens * depth * width,
        4 * depth * width,
        args,
        aliases,
    )


def token_sums(halves, columns, orders):
    position = lax.axis_index("col")
    bits = len(orders[0])
    rows = halves[0].shape[0] // columns
    halves = [half.reshape((2,) * bits + (rows, half.shape[1])) for half in halves]
    lefts = [list(reversed(range(bits))) for _ in halves]
    stages = []
    for stage in range(bits):
        kept, got = [], []
        for half, left, order in zip(halves, lefts, orders):
            bit = order[stage]
            axis = left.index(bit)
            left.remove(bit)
            mine = (position // 2**bit) % 2
            send = lax.dynamic_index_in_dim(half, 1 - mine, axis, keepdims=False)
            moves = [(c, c ^ 2**bit) for c in range(columns)]
            got.append(lax.ppermute(send.astype(BF16), "col", moves))
            kept.append(lax.dynamic_index_in_dim(half, mine, axis, keepdims=False))
        halves = [keep + far.astype(F32) for keep, far in zip(kept, got)]
        stages.append(halves)
    return stages


def local(quarters, columns, inputs, gate_weight, up_weight, hidden_grad):
    outer = quarters // 2
    full = gate_weight.shape[1]
    block, chunks = chunk_list(full)
    swap = [(r, r ^ 1) for r in range(quarters)]

    def sibling(value):
        return lax.ppermute(value, "row", swap)

    def across(value, step):
        moves = [(r, (r // 2 + step) % outer * 2 + r % 2) for r in range(quarters)]
        return lax.ppermute(value, "row", moves)

    owns, gots, sums = [], [], []
    for i, (start, count) in enumerate(chunks):
        after = sums[i - 2][:1] if i >= 2 else []
        own, far, send = forward_part(
            quarters, block, start, count, inputs, gate_weight, up_weight, after
        )
        got = sibling(send)
        owns.append(own)
        gots.append(got)
        sums.append(
            [(far[step - 1] + got[step].astype(F32)).astype(BF16) for step in range(1, outer)]
        )

    xt = inputs.T
    hidden = None
    pieces = []
    for (start, count), own, got, near in zip(chunks, owns, gots, sums):
        far = [across(value, step + 1) for step, value in enumerate(near)]
        at = slice(start * block, (start + count) * block)
        hidden, mine = middle_part(outer, at, own, got, far, hidden_grad, hidden)
        group = [mine, sibling(mine)]
        for step in range(1, outer):
            there = across(mine, step)
            group += [there, sibling(there)]
        pieces.append(group)

    acc = None
    grads = []
    for (start, count), group in zip(chunks, pieces):
        acc, whole = input_part(
            quarters, block, start, count, gate_weight, up_weight, group, acc
        )
        grads.append(whole)
    bits = columns.bit_length() - 1
    order = list(range(bits))
    stages = [acc] + token_sums(acc, columns, [order, order[1::-1] + order[2:]])
    input_grad = jnp.concatenate([half.astype(BF16) for half in stages[-1]], axis=1)
    state = []
    for i, ((start, count), whole) in enumerate(zip(chunks, grads)):
        after = stages[min(i, bits) - 1] if i else []
        state = weight_part(block, start, count, full, xt, whole, state, after)
    return hidden, input_grad, state[0], state[1]


def solution(mesh):
    return jax.shard_map(
        functools.partial(local, mesh.shape["row"], mesh.shape["col"]),
        mesh=mesh,
        in_specs=(P(None, "row"), P("row", "col"), P("row", "col"), P("row", "col")),
        out_specs=(P("row", "col"), P("col", "row"), P("row", "col"), P("row", "col")),
        check_vma=False,
    )
```

```python
import functools

import jax
import jax.numpy as jnp
from jax import lax
from jax.experimental import pallas as pl
from jax.experimental.pallas import tpu as pltpu
from jax.sharding import PartitionSpec as P

BF16 = jnp.bfloat16
F32 = jnp.float32
VMEM_BYTES = 12 * 1024 * 1024
SHARES = (2, 4, 5, 3)
SLOTS = 4
WHOLE = pl.BlockSpec(memory_space=pltpu.VMEM)
REMOTE = pl.BlockSpec(memory_space=pl.ANY)


def chunk_list(width):
    block = 256 if width % 256 == 0 else 128
    units = width // block
    total = sum(SHARES)
    edges = [0]
    run = 0
    for share in SHARES:
        run += share
        edges.append(max(min(units, round(units * run / total)), edges[-1]))
    return block, [(a, b - a) for a, b in zip(edges, edges[1:]) if b > a]


def call(kernel, name, in_specs, out_specs, out_shape, scratch, args, aliases=None):
    return pl.pallas_call(
        kernel,
        in_specs=in_specs,
        out_specs=out_specs,
        out_shape=out_shape,
        scratch_shapes=scratch,
        input_output_aliases=aliases or {},
        compiler_params=pltpu.CompilerParams(vmem_limit_bytes=VMEM_BYTES),
        cost_estimate=pl.CostEstimate(flops=1000, bytes_accessed=1000, transcendentals=0),
        name=name,
    )(*args)


def in_hbm(value):
    return pltpu.with_memory_space_constraint(value, pltpu.HBM)


def fetches(sources, columns, targets, sems):
    depth = sources[0].shape[0]
    parts = sems.shape[1]
    deep = depth // parts
    return [
        pltpu.make_async_copy(
            source.at[pl.ds(p * deep, deep), columns],
            target.at[pl.ds(p * deep, deep)],
            sems.at[k, p],
        )
        for p in range(parts)
        for k, (source, target) in enumerate(zip(sources, targets))
    ]


def forward_kernel(layout, ins, outs, *refs):
    quarters, rows, block, own_at, next_at = layout
    given, made, (total, own_sems, next_sems) = refs[:ins], refs[ins : ins + outs], refs[ins + outs :]
    x_ref, gate_ref, up_ref = given[:3]
    own_ref, far_ref, send_ref, *made = made
    start = []
    if own_at is None:
        weights = given[3:5]
    else:
        start = fetches((gate_ref, up_ref), own_at, made[1:3], own_sems)
        start.append(pltpu.make_async_copy(x_ref, made[0], next_sems.at[2, 0]))
        for copy in start:
            copy.start()
        x_ref, weights, made = made[0], made[1:3], made[3:]
    later = []
    if next_at is not None:
        later = fetches((gate_ref, up_ref), next_at, made, next_sems.at[:2])
    for copy in start:
        copy.wait()
    for copy in later:
        copy.start()
    outer = quarters // 2
    me = lax.axis_index("row")
    place, core = me // 2, me % 2
    x = x_ref[...]
    for j in range(weights[0].shape[1] // block):
        at = slice(j * block, (j + 1) * block)
        for k in range(2):
            total[k] = jnp.dot(x, weights[k][:, at], preferred_element_type=F32)
        for step in range(outer):
            there = (place + step) % outer * 2
            mine = pl.multiple_of((there + core) * rows, rows)
            other = pl.multiple_of((there + 1 - core) * rows, rows)
            for k in range(2):
                kept = total[k, pl.ds(mine, rows), :]
                if step == 0:
                    own_ref[k, :, at] = kept
                else:
                    far_ref[step - 1, k, :, at] = kept
                send_ref[step, k, :, at] = total[k, pl.ds(other, rows), :].astype(BF16)
    for copy in later:
        copy.wait()


def forward_part(quarters, block, chunk, following, x, gate_weight, up_weight, held, after):
    tokens, depth = x.shape
    rows = tokens // quarters
    outer = quarters // 2
    width = chunk[1] * block
    own_at = None if held else pl.ds(chunk[0] * block, width)
    next_at = None
    out_shape = [
        jax.ShapeDtypeStruct((2, rows, width), F32),
        jax.ShapeDtypeStruct((outer - 1, 2, rows, width), F32),
        jax.ShapeDtypeStruct((outer, 2, rows, width), BF16),
    ]
    if not held:
        x = pltpu.with_memory_space_constraint(x, pltpu.HBM)
        out_shape += [pltpu.VMEM(x.shape, BF16)] + [pltpu.VMEM((depth, width), BF16)] * 2
    if following is not None:
        next_at = pl.ds(following[0] * block, following[1] * block)
        out_shape += [pltpu.VMEM((depth, following[1] * block), BF16)] * 2
    args = (x, in_hbm(gate_weight), in_hbm(up_weight), *held, *after)
    parts = 4 if depth % 512 == 0 else 2
    own, far, send, *loaded = call(
        functools.partial(
            forward_kernel,
            (quarters, rows, block, own_at, next_at),
            len(args),
            len(out_shape),
        ),
        "forward_part",
        [WHOLE if held else REMOTE, REMOTE, REMOTE] + [WHOLE] * len(held) + [REMOTE] * len(after),
        [WHOLE] * len(out_shape),
        out_shape,
        [
            pltpu.VMEM((2, tokens, block), F32),
            pltpu.SemaphoreType.DMA((2, parts)),
            pltpu.SemaphoreType.DMA((3, parts)),
        ],
        args,
    )
    return own, far, send, loaded


def middle_kernel(outer, at, first, own_ref, got_ref, upstream_ref, *refs):
    far_refs, rest = refs[: outer - 1], refs[outer - 1 :]
    if not first:
        rest[1][...] = rest[0][...]
        rest = rest[1:]
    hidden_ref, grads_ref = rest
    gate_pre = own_ref[0] + got_ref[0, 0].astype(F32)
    up_pre = own_ref[1] + got_ref[0, 1].astype(F32)
    for far in far_refs:
        gate_pre += far[0].astype(F32)
        up_pre += far[1].astype(F32)
    sigma_gate = jax.nn.sigmoid(gate_pre)
    upstream = upstream_ref[:, at].astype(F32)
    gated = gate_pre * sigma_gate
    hidden_ref[:, at] = (gated * up_pre).astype(BF16)
    slope = sigma_gate * (1.0 + gate_pre * (1.0 - sigma_gate))
    grads_ref[0] = (upstream * up_pre * slope).astype(BF16)
    grads_ref[1] = (upstream * gated).astype(BF16)


def middle_part(outer, at, own, got, far, hidden_grad, hidden):
    rows, width = own.shape[1:]
    first = hidden is None
    args = [own, got, hidden_grad, *far] + ([] if first else [hidden])
    return call(
        functools.partial(middle_kernel, outer, at, first),
        "middle_part",
        [WHOLE] * len(args),
        [WHOLE] * 2,
        [
            jax.ShapeDtypeStruct(hidden_grad.shape, BF16),
            jax.ShapeDtypeStruct((2, rows, width), BF16),
        ],
        [],
        args,
    )


def input_kernel(quarters, rows, first, last, gate_ref, up_ref, *refs):
    pieces, rest = refs[:quarters], refs[quarters:]
    earlier = []
    if not first:
        count = 2 if last else 1
        earlier, rest = rest[:count], rest[count:]
    *sums, grads = rest
    outer = quarters // 2
    me = lax.axis_index("row")
    place, core = me // 2, me % 2
    for j, piece in enumerate(pieces):
        step, swap = j // 2, j % 2
        there = (place + outer - step) % outer * 2
        at = pl.multiple_of((there + (core + swap) % 2) * rows, rows)
        for k in range(2):
            grads[k, pl.ds(at, rows), :] = piece[k]
    weights = (gate_ref, up_ref)
    deep = 256 if gate_ref.shape[0] % 512 == 0 else 128
    if last:
        dims = (((1,), (1,)), ((), ()))
        half = sums[0].shape[1]
        for d in range(gate_ref.shape[0] // deep):
            index, at = d * deep // half, slice(d * deep % half, d * deep % half + deep)
            term = None if first else earlier[index][:, at]
            for k in range(2):
                piece = weights[k][d * deep : (d + 1) * deep, :]
                product = lax.dot_general(grads[k], piece, dims, preferred_element_type=F32)
                term = product if term is None else term + product
            sums[index][:, at] = term
        return
    flipped = [grads[k].T for k in range(2)]
    for d in range(gate_ref.shape[0] // deep):
        at = slice(d * deep, (d + 1) * deep)
        term = None if first else earlier[0][at, :]
        for k in range(2):
            product = jnp.dot(weights[k][at, :], flipped[k], preferred_element_type=F32)
            term = product if term is None else term + product
        if len(sums) == 1:
            sums[0][at, :] = term
        else:
            half = sums[0].shape[1]
            sums[d * deep // half][:, d * deep % half : d * deep % half + deep] = term.T


def input_part(quarters, held, pieces, acc, final):
    depth, width = held[0].shape
    rows = pieces[0].shape[1]
    tokens = rows * quarters
    first, last = acc is None, final == 0
    args = [*held, *pieces] + ([] if first else acc)
    sums = [jax.ShapeDtypeStruct((depth, tokens), F32)]
    if final <= 1:
        sums = [jax.ShapeDtypeStruct((tokens, depth // 2), F32)] * 2
    *acc, grads = call(
        functools.partial(input_kernel, quarters, rows, first, last),
        "input_part",
        [WHOLE] * len(args),
        [WHOLE] * (len(sums) + 1),
        sums + [jax.ShapeDtypeStruct((2, tokens, width), BF16)],
        [],
        args,
    )
    return acc, grads


def weight_kernel(block, start, count, skipped, xt_ref, grads_ref, *refs):
    gate_out, up_out, products, sems = refs[skipped:]
    xt = xt_ref[...]
    slots = products.shape[0]
    copies = []
    for j in range(count):
        for k, out in enumerate((gate_out, up_out)):
            piece = grads_ref[k, :, j * block : (j + 1) * block]
            slot = len(copies) % slots
            if len(copies) >= slots:
                copies[-slots].wait()
            products[slot] = jnp.dot(xt, piece, preferred_element_type=F32).astype(BF16)
            copy = pltpu.make_async_copy(
                products.at[slot], out.at[:, pl.ds((start + j) * block, block)], sems.at[slot]
            )
            copy.start()
            copies.append(copy)
    for copy in copies[-slots:]:
        copy.wait()


def weight_part(block, start, count, full, xt, grads, state, after):
    depth, tokens = xt.shape
    args = [xt, grads, *after, *[in_hbm(value) for value in state]]
    first = 2 + len(after)
    aliases = {first + k: k for k in range(len(state))}
    return call(
        functools.partial(weight_kernel, block, start, count, len(args) - 2),
        "weight_part",
        [WHOLE] * 2 + [REMOTE] * (len(args) - 2),
        [REMOTE] * 2,
        [pltpu.HBM((depth, full), BF16)] * 2,
        [pltpu.VMEM((SLOTS, depth, block), BF16), pltpu.SemaphoreType.DMA((SLOTS,))],
        args,
        aliases,
    )


def token_sums(halves, columns, orders):
    position = lax.axis_index("col")
    bits = len(orders[0])
    rows = halves[0].shape[0] // columns
    halves = [half.reshape((2,) * bits + (rows, half.shape[1])) for half in halves]
    lefts = [list(reversed(range(bits))) for _ in halves]
    stages = []
    for stage in range(bits):
        kept, got = [], []
        for half, left, order in zip(halves, lefts, orders):
            bit = order[stage]
            axis = left.index(bit)
            left.remove(bit)
            mine = (position // 2**bit) % 2
            send = lax.dynamic_index_in_dim(half, 1 - mine, axis, keepdims=False)
            moves = [(c, c ^ 2**bit) for c in range(columns)]
            got.append(lax.ppermute(send.astype(BF16), "col", moves))
            kept.append(lax.dynamic_index_in_dim(half, mine, axis, keepdims=False))
        halves = [keep + far.astype(F32) for keep, far in zip(kept, got)]
        stages.append(halves)
    return stages


def local(quarters, columns, inputs, gate_weight, up_weight, hidden_grad):
    outer = quarters // 2
    full = gate_weight.shape[1]
    block, chunks = chunk_list(full)
    swap = [(r, r ^ 1) for r in range(quarters)]

    def sibling(value):
        return lax.ppermute(value, "row", swap)

    def across(value, step):
        moves = [(r, (r // 2 + step) % outer * 2 + r % 2) for r in range(quarters)]
        return lax.ppermute(value, "row", moves)

    owns, gots, sums, weights = [], [], [], []
    x = inputs
    for i, chunk in enumerate(chunks):
        after = sums[i - 2][:1] if i >= 2 else []
        following = chunks[i + 1] if i + 1 < len(chunks) else None
        held = weights[i] if i else []
        own, far, send, loaded = forward_part(
            quarters, block, chunk, following, x, gate_weight, up_weight, held, after
        )
        if i == 0:
            x, loaded = loaded[0], loaded[1:]
        while loaded:
            weights.append(loaded[:2])
            loaded = loaded[2:]
        got = sibling(send)
        owns.append(own)
        gots.append(got)
        sums.append(
            [(far[step - 1] + got[step].astype(F32)).astype(BF16) for step in range(1, outer)]
        )

    xt = x.T
    hidden = None
    pieces = []
    for (start, count), own, got, near in zip(chunks, owns, gots, sums):
        far = [across(value, step + 1) for step, value in enumerate(near)]
        at = slice(start * block, (start + count) * block)
        hidden, mine = middle_part(outer, at, own, got, far, hidden_grad, hidden)
        group = [mine, sibling(mine)]
        for step in range(1, outer):
            there = across(mine, step)
            group += [there, sibling(there)]
        pieces.append(group)

    acc = None
    grads = []
    for i, (held, group) in enumerate(zip(weights, pieces)):
        acc, whole = input_part(quarters, held, group, acc, len(chunks) - 1 - i)
        grads.append(whole)
    bits = columns.bit_length() - 1
    order = list(range(bits))
    stages = [acc] + token_sums(acc, columns, [order, order[1::-1] + order[2:]])
    input_grad = jnp.concatenate([half.astype(BF16) for half in stages[-1]], axis=1)
    state = []
    for i, ((start, count), whole) in enumerate(zip(chunks, grads)):
        after = stages[min(i, bits) - 1] if i else []
        state = weight_part(block, start, count, full, xt, whole, state, after)
    return hidden, input_grad, state[0], state[1]


def solution(mesh):
    return jax.shard_map(
        functools.partial(local, mesh.shape["row"], mesh.shape["col"]),
        mesh=mesh,
        in_specs=(P(None, "row"), P("row", "col"), P("row", "col"), P("row", "col")),
        out_specs=(P("row", "col"), P("col", "row"), P("row", "col"), P("row", "col")),
        check_vma=False,
    )
```

```python
import functools

import jax
import jax.numpy as jnp
from jax import lax
from jax.experimental import pallas as pl
from jax.experimental.pallas import tpu as pltpu
from jax.sharding import PartitionSpec as P

BF16 = jnp.bfloat16
F32 = jnp.float32
VMEM_BYTES = 8 * 1024 * 1024
SHARES = (2, 4, 5, 3)
SLOTS = 4
COST = 40
WHOLE = pl.BlockSpec(memory_space=pltpu.VMEM)
REMOTE = pl.BlockSpec(memory_space=pl.ANY)


def chunk_list(width):
    block = 256 if width % 256 == 0 else 128
    units = width // block
    total = sum(SHARES)
    edges = [0]
    run = 0
    for share in SHARES:
        run += share
        edges.append(max(min(units, round(units * run / total)), edges[-1]))
    return block, [(a, b - a) for a, b in zip(edges, edges[1:]) if b > a]


def call(kernel, name, in_specs, out_specs, out_shape, scratch, size, args, aliases=None):
    return pl.pallas_call(
        kernel,
        in_specs=in_specs,
        out_specs=out_specs,
        out_shape=out_shape,
        scratch_shapes=scratch,
        input_output_aliases=aliases or {},
        compiler_params=pltpu.CompilerParams(vmem_limit_bytes=VMEM_BYTES),
        cost_estimate=pl.CostEstimate(
            flops=COST * size, bytes_accessed=size, transcendentals=0
        ),
        name=name,
    )(*args)


def in_hbm(value):
    return pltpu.with_memory_space_constraint(value, pltpu.HBM)


def forward_kernel(layout, ins, outs, *refs):
    quarters, rows, block, start, count, following, first = layout
    given, made, (total, sems, x_sem) = refs[:ins], refs[ins : ins + outs], refs[ins + outs :]
    sources = given[1:3]
    own_ref, far_ref, send_ref, *made = made
    x_ref, early = given[0], given[3:5]
    folds = []
    if first:
        x_copy = pltpu.make_async_copy(x_ref, made[0], x_sem)
        x_copy.start()
        x_ref, made = made[0], made[1:]
    weights, ahead = made[:2], made[2:]
    queue = [
        [
            pltpu.make_async_copy(
                source.at[:, pl.ds((start + j) * block, block)],
                target.at[:, pl.ds(j * block, block)],
                sems.at[k, j],
            )
            for k, (source, target) in enumerate(zip(sources, weights))
        ]
        for j in range(0 if first else 1, count)
    ]
    if ahead:
        queue.append(
            [
                pltpu.make_async_copy(
                    source.at[:, pl.ds(following * block, block)], target, sems.at[k, count]
                )
                for k, (source, target) in enumerate(zip(sources, ahead))
            ]
        )
    for pair in queue[:2]:
        for copy in pair:
            copy.start()
    if first:
        x_copy.wait()
    else:
        folds = [
            pltpu.make_async_copy(early[k], weights[k].at[:, pl.ds(0, block)], sems.at[k, 0])
            for k in range(2)
        ]
        for copy in folds:
            copy.start()
    outer = quarters // 2
    me = lax.axis_index("row")
    place, core = me // 2, me % 2
    x = x_ref[...]
    taken = 0
    for j in range(count):
        at = slice(j * block, (j + 1) * block)
        if first or j:
            for copy in queue[taken]:
                copy.wait()
            taken += 1
            for copy in queue[taken + 1] if taken + 1 < len(queue) else []:
                copy.start()
            blocks = [ref[:, at] for ref in weights]
        else:
            blocks = [ref[...] for ref in early]
        for k in range(2):
            total[k] = jnp.dot(x, blocks[k], preferred_element_type=F32)
        for step in range(outer):
            there = (place + step) % outer * 2
            mine = pl.multiple_of((there + core) * rows, rows)
            other = pl.multiple_of((there + 1 - core) * rows, rows)
            for k in range(2):
                kept = total[k, pl.ds(mine, rows), :]
                if step == 0:
                    own_ref[k, :, at] = kept
                else:
                    far_ref[step - 1, k, :, at] = kept
                send_ref[step, k, :, at] = total[k, pl.ds(other, rows), :].astype(BF16)
    for copy in folds:
        copy.wait()
    for pair in queue[taken:]:
        for copy in pair:
            copy.wait()


def forward_part(quarters, block, chunk, following, x, gate_weight, up_weight, early, after):
    tokens, depth = x.shape
    rows = tokens // quarters
    outer = quarters // 2
    start, count = chunk
    width = count * block
    first = not early
    out_shape = [
        jax.ShapeDtypeStruct((2, rows, width), F32),
        jax.ShapeDtypeStruct((outer - 1, 2, rows, width), F32),
        jax.ShapeDtypeStruct((outer, 2, rows, width), BF16),
    ]
    if first:
        x = in_hbm(x)
        out_shape.append(pltpu.VMEM(x.shape, BF16))
    out_shape += [pltpu.VMEM((depth, width), BF16)] * 2
    if following is not None:
        out_shape += [pltpu.VMEM((depth, block), BF16)] * 2
    args = (x, in_hbm(gate_weight), in_hbm(up_weight), *early, *after)
    layout = (quarters, rows, block, start, count, following, first)
    return call(
        functools.partial(forward_kernel, layout, len(args), len(out_shape)),
        "forward_part",
        [REMOTE if first else WHOLE, REMOTE, REMOTE]
        + [WHOLE] * len(early)
        + [REMOTE] * len(after),
        [WHOLE] * len(out_shape),
        out_shape,
        [
            pltpu.VMEM((2, tokens, block), F32),
            pltpu.SemaphoreType.DMA((2, count + 1)),
            pltpu.SemaphoreType.DMA,
        ],
        tokens * depth * width,
        args,
    )


def middle_kernel(outer, at, first, skipped, own_ref, got_ref, upstream_ref, *refs):
    far_refs, rest = refs[: outer - 1], refs[outer - 1 + skipped :]
    if not first:
        rest[1][...] = rest[0][...]
        rest = rest[1:]
    hidden_ref, grads_ref = rest
    gate_pre = own_ref[0] + got_ref[0, 0].astype(F32)
    up_pre = own_ref[1] + got_ref[0, 1].astype(F32)
    for far in far_refs:
        gate_pre += far[0].astype(F32)
        up_pre += far[1].astype(F32)
    sigma_gate = jax.nn.sigmoid(gate_pre)
    upstream = upstream_ref[:, at].astype(F32)
    gated = gate_pre * sigma_gate
    hidden_ref[:, at] = (gated * up_pre).astype(BF16)
    slope = sigma_gate * (1.0 + gate_pre * (1.0 - sigma_gate))
    grads_ref[0] = (upstream * up_pre * slope).astype(BF16)
    grads_ref[1] = (upstream * gated).astype(BF16)


def middle_part(outer, at, own, got, far, hidden_grad, hidden, after):
    rows, width = own.shape[1:]
    first = hidden is None
    args = [own, got, hidden_grad, *far, *after] + ([] if first else [hidden])
    return call(
        functools.partial(middle_kernel, outer, at, first, len(after)),
        "middle_part",
        [WHOLE] * (2 + outer) + [REMOTE] * len(after) + [WHOLE] * (not first),
        [WHOLE] * 2,
        [
            jax.ShapeDtypeStruct(hidden_grad.shape, BF16),
            jax.ShapeDtypeStruct((2, rows, width), BF16),
        ],
        [],
        rows * width,
        args,
    )


def input_kernel(quarters, rows, first, last, skipped, gate_ref, up_ref, *refs):
    pieces, rest = refs[:quarters], refs[quarters + skipped :]
    earlier = []
    if not first:
        count = 2 if last else 1
        earlier, rest = rest[:count], rest[count:]
    *sums, grads = rest
    outer = quarters // 2
    me = lax.axis_index("row")
    place, core = me // 2, me % 2
    for j, piece in enumerate(pieces):
        step, swap = j // 2, j % 2
        there = (place + outer - step) % outer * 2
        at = pl.multiple_of((there + (core + swap) % 2) * rows, rows)
        for k in range(2):
            grads[k, pl.ds(at, rows), :] = piece[k]
    weights = (gate_ref, up_ref)
    deep = 256 if gate_ref.shape[0] % 512 == 0 else 128
    if last:
        dims = (((1,), (1,)), ((), ()))
        half = sums[0].shape[1]
        for d in range(gate_ref.shape[0] // deep):
            index, at = d * deep // half, slice(d * deep % half, d * deep % half + deep)
            term = None if first else earlier[index][:, at]
            for k in range(2):
                piece = weights[k][d * deep : (d + 1) * deep, :]
                product = lax.dot_general(grads[k], piece, dims, preferred_element_type=F32)
                term = product if term is None else term + product
            sums[index][:, at] = term
        return
    flipped = [grads[k].T for k in range(2)]
    for d in range(gate_ref.shape[0] // deep):
        at = slice(d * deep, (d + 1) * deep)
        term = None if first else earlier[0][at, :]
        for k in range(2):
            product = jnp.dot(weights[k][at, :], flipped[k], preferred_element_type=F32)
            term = product if term is None else term + product
        if len(sums) == 1:
            sums[0][at, :] = term
        else:
            half = sums[0].shape[1]
            sums[d * deep // half][:, d * deep % half : d * deep % half + deep] = term.T


def input_part(quarters, held, pieces, acc, final, after):
    depth, width = held[0].shape
    rows = pieces[0].shape[1]
    tokens = rows * quarters
    first, last = acc is None, final == 0
    args = [*held, *pieces, *after] + ([] if first else acc)
    sums = [jax.ShapeDtypeStruct((depth, tokens), F32)]
    if final <= 1:
        sums = [jax.ShapeDtypeStruct((tokens, depth // 2), F32)] * 2
    *acc, grads = call(
        functools.partial(input_kernel, quarters, rows, first, last, len(after)),
        "input_part",
        [WHOLE] * (2 + quarters) + [REMOTE] * len(after) + [WHOLE] * (0 if first else len(acc)),
        [WHOLE] * (len(sums) + 1),
        sums + [jax.ShapeDtypeStruct((2, tokens, width), BF16)],
        [],
        tokens * depth * width,
        args,
    )
    return acc, grads


def weight_kernel(block, start, count, skipped, xt_ref, grads_ref, *refs):
    gate_out, up_out, products, sems = refs[skipped:]
    xt = xt_ref[...]
    slots = products.shape[0]
    copies = []
    for j in range(count):
        for k, out in enumerate((gate_out, up_out)):
            piece = grads_ref[k, :, j * block : (j + 1) * block]
            slot = len(copies) % slots
            if len(copies) >= slots:
                copies[-slots].wait()
            products[slot] = jnp.dot(xt, piece, preferred_element_type=F32).astype(BF16)
            copy = pltpu.make_async_copy(
                products.at[slot], out.at[:, pl.ds((start + j) * block, block)], sems.at[slot]
            )
            copy.start()
            copies.append(copy)
    for copy in copies[-slots:]:
        copy.wait()


def weight_part(block, start, count, full, xt, grads, state, after):
    depth, tokens = xt.shape
    args = [xt, grads, *after, *[in_hbm(value) for value in state]]
    first = 2 + len(after)
    aliases = {first + k: k for k in range(len(state))}
    return call(
        functools.partial(weight_kernel, block, start, count, len(args) - 2),
        "weight_part",
        [WHOLE] * 2 + [REMOTE] * (len(args) - 2),
        [REMOTE] * 2,
        [pltpu.HBM((depth, full), BF16)] * 2,
        [pltpu.VMEM((SLOTS, depth, block), BF16), pltpu.SemaphoreType.DMA((SLOTS,))],
        tokens * depth * count * block,
        args,
        aliases,
    )


def token_sums(halves, columns, orders):
    position = lax.axis_index("col")
    bits = len(orders[0])
    rows = halves[0].shape[0] // columns
    halves = [half.reshape((2,) * bits + (rows, half.shape[1])) for half in halves]
    lefts = [list(reversed(range(bits))) for _ in halves]
    stages = []
    for stage in range(bits):
        kept, got = [], []
        for half, left, order in zip(halves, lefts, orders):
            bit = order[stage]
            axis = left.index(bit)
            left.remove(bit)
            mine = (position // 2**bit) % 2
            send = lax.dynamic_index_in_dim(half, 1 - mine, axis, keepdims=False)
            moves = [(c, c ^ 2**bit) for c in range(columns)]
            got.append(lax.ppermute(send.astype(BF16), "col", moves))
            kept.append(lax.dynamic_index_in_dim(half, mine, axis, keepdims=False))
        halves = [keep + far.astype(F32) for keep, far in zip(kept, got)]
        stages.append(halves)
    return stages


def local(quarters, columns, inputs, gate_weight, up_weight, hidden_grad):
    outer = quarters // 2
    full = gate_weight.shape[1]
    block, chunks = chunk_list(full)
    swap = [(r, r ^ 1) for r in range(quarters)]

    def sibling(value):
        return lax.ppermute(value, "row", swap)

    def across(value, step):
        moves = [(r, (r // 2 + step) % outer * 2 + r % 2) for r in range(quarters)]
        return lax.ppermute(value, "row", moves)

    def forward(i, x, early, after):
        following = chunks[i + 1][0] if i + 1 < len(chunks) else None
        own, far, send, *loaded = forward_part(
            quarters, block, chunks[i], following, x, gate_weight, up_weight, early, after
        )
        if i == 0:
            x, loaded = loaded[0], loaded[1:]
        weights.append(loaded[:2])
        got = sibling(send)
        near = [(far[step - 1] + got[step].astype(F32)).astype(BF16) for step in range(1, outer)]
        owns.append(own)
        gots.append(got)
        sums.append(near)
        crossed.append([across(value, step + 1) for step, value in enumerate(near)])
        return x, loaded[2:]

    def middle(i, hidden, after):
        start, count = chunks[i]
        at = slice(start * block, (start + count) * block)
        hidden, mine = middle_part(
            outer, at, owns[i], gots[i], crossed[i], hidden_grad, hidden, after
        )
        group = [mine, sibling(mine)]
        for step in range(1, outer):
            there = across(mine, step)
            group += [there, sibling(there)]
        pieces.append(group)
        return hidden

    weights, owns, gots, sums, crossed, pieces = [], [], [], [], [], []
    number = len(chunks)
    x, early, hidden = inputs, [], None
    for i in range(number):
        after = []
        if i >= 2:
            after = sums[i - 2][:1]
        if i >= 3:
            hidden = middle(i - 3, hidden, [])
            after = after + [pieces[i - 3][0]]
        x, early = forward(i, x, early, after)
    for i in range(max(number - 3, 0), number):
        hidden = middle(i, hidden, pieces[i - 2][2:3] if i >= 2 else [])

    xt = x.T
    bits = columns.bit_length() - 1
    order = list(range(bits))
    acc, state = None, []
    grads = []
    for i in range(number):
        after = state[:1] if i == number - 1 else []
        acc, whole = input_part(quarters, weights[i], pieces[i], acc, number - 1 - i, after)
        grads.append(whole)
        if i < number - 2:
            state = weight_part(block, *chunks[i], full, xt, whole, state, [])
    stages = [acc] + token_sums(acc, columns, [order, order[1::-1] + order[2:]])
    input_grad = jnp.concatenate([half.astype(BF16) for half in stages[-1]], axis=1)
    for i in range(max(number - 2, 0), number):
        after = stages[min(i - max(number - 2, 0), bits)]
        state = weight_part(block, *chunks[i], full, xt, grads[i], state, after)
    return hidden, input_grad, state[0], state[1]


def solution(mesh):
    return jax.shard_map(
        functools.partial(local, mesh.shape["row"], mesh.shape["col"]),
        mesh=mesh,
        in_specs=(P(None, "row"), P("row", "col"), P("row", "col"), P("row", "col")),
        out_specs=(P("row", "col"), P("col", "row"), P("row", "col"), P("row", "col")),
        check_vma=False,
    )
```

```python
import functools

import jax
import jax.numpy as jnp
from jax import lax
from jax.experimental import pallas as pl
from jax.experimental.pallas import tpu as pltpu
from jax.sharding import PartitionSpec as P

BF16 = jnp.bfloat16
F32 = jnp.float32
VMEM_BYTES = 16 * 1024 * 1024
SHARES = (2, 4, 5, 3)
SLOTS = 3
COST = 40
WHOLE = pl.BlockSpec(memory_space=pltpu.VMEM)
REMOTE = pl.BlockSpec(memory_space=pl.ANY)


def chunk_list(width):
    block = 256 if width % 256 == 0 else 128
    units = width // block
    total = sum(SHARES)
    edges = [0]
    run = 0
    for share in SHARES:
        run += share
        edges.append(max(min(units, round(units * run / total)), edges[-1]))
    return block, [(a, b - a) for a, b in zip(edges, edges[1:]) if b > a]


def call(kernel, name, in_specs, out_specs, out_shape, scratch, size, args, aliases=None):
    return pl.pallas_call(
        kernel,
        in_specs=in_specs,
        out_specs=out_specs,
        out_shape=out_shape,
        scratch_shapes=scratch,
        input_output_aliases=aliases or {},
        compiler_params=pltpu.CompilerParams(vmem_limit_bytes=VMEM_BYTES),
        cost_estimate=pl.CostEstimate(
            flops=COST * size, bytes_accessed=size, transcendentals=0
        ),
        name=name,
    )(*args)


def in_hbm(value):
    return pltpu.with_memory_space_constraint(value, pltpu.HBM)


def forward_kernel(layout, ins, outs, *refs):
    quarters, rows, block, start, count, following, first = layout
    given, made = refs[:ins], refs[ins : ins + outs]
    weights, total, sems, x_sem = refs[ins + outs :]
    sources = given[1:3]
    own_ref, far_ref, send_ref, *made = made
    x_ref, early = given[0], given[3:5]
    if first:
        x_copy = pltpu.make_async_copy(x_ref, made[0], x_sem)
        x_copy.start()
        x_ref, made = made[0], made[1:]
    slots = weights.shape[1]
    queue = [
        [
            pltpu.make_async_copy(
                source.at[:, pl.ds((start + j) * block, block)],
                weights.at[k, j % slots],
                sems.at[k, j % slots],
            )
            for k, source in enumerate(sources)
        ]
        for j in range(0 if first else 1, count)
    ]
    if made:
        queue.append(
            [
                pltpu.make_async_copy(
                    source.at[:, pl.ds(following * block, block)], target, sems.at[k, slots]
                )
                for k, (source, target) in enumerate(zip(sources, made))
            ]
        )
    for pair in queue[:2]:
        for copy in pair:
            copy.start()
    if first:
        x_copy.wait()
    outer = quarters // 2
    me = lax.axis_index("row")
    place, core = me // 2, me % 2
    x = x_ref[...]
    taken = 0
    for j in range(count):
        at = slice(j * block, (j + 1) * block)
        if first or j:
            for copy in queue[taken]:
                copy.wait()
            taken += 1
            for copy in queue[taken + 1] if taken + 1 < len(queue) else []:
                copy.start()
            blocks = [weights[k, j % slots] for k in range(2)]
        else:
            blocks = [ref[...] for ref in early]
        for k in range(2):
            total[k] = jnp.dot(x, blocks[k], preferred_element_type=F32)
        for step in range(outer):
            there = (place + step) % outer * 2
            mine = pl.multiple_of((there + core) * rows, rows)
            other = pl.multiple_of((there + 1 - core) * rows, rows)
            for k in range(2):
                kept = total[k, pl.ds(mine, rows), :]
                if step == 0:
                    own_ref[k, :, at] = kept
                else:
                    far_ref[step - 1, k, :, at] = kept
                send_ref[step, k, :, at] = total[k, pl.ds(other, rows), :].astype(BF16)
    for pair in queue[taken:]:
        for copy in pair:
            copy.wait()


def forward_part(quarters, block, chunk, following, x, gate_weight, up_weight, early, after):
    tokens, depth = x.shape
    rows = tokens // quarters
    outer = quarters // 2
    start, count = chunk
    width = count * block
    first = not early
    out_shape = [
        jax.ShapeDtypeStruct((2, rows, width), F32),
        jax.ShapeDtypeStruct((outer - 1, 2, rows, width), F32),
        jax.ShapeDtypeStruct((outer, 2, rows, width), BF16),
    ]
    if first:
        x = in_hbm(x)
        out_shape.append(pltpu.VMEM(x.shape, BF16))
    if following is not None:
        out_shape += [pltpu.VMEM((depth, block), BF16)] * 2
    args = (x, in_hbm(gate_weight), in_hbm(up_weight), *early, *after)
    layout = (quarters, rows, block, start, count, following, first)
    return call(
        functools.partial(forward_kernel, layout, len(args), len(out_shape)),
        "forward_part",
        [REMOTE if first else WHOLE, REMOTE, REMOTE]
        + [WHOLE] * len(early)
        + [REMOTE] * len(after),
        [WHOLE] * len(out_shape),
        out_shape,
        [
            pltpu.VMEM((2, SLOTS, depth, block), BF16),
            pltpu.VMEM((2, tokens, block), F32),
            pltpu.SemaphoreType.DMA((2, SLOTS + 1)),
            pltpu.SemaphoreType.DMA,
        ],
        tokens * depth * width,
        args,
    )


def middle_kernel(outer, at, first, skipped, own_ref, got_ref, upstream_ref, *refs):
    far_refs, rest = refs[: outer - 1], refs[outer - 1 + skipped :]
    if not first:
        rest[1][...] = rest[0][...]
        rest = rest[1:]
    hidden_ref, grads_ref = rest
    gate_pre = own_ref[0] + got_ref[0, 0].astype(F32)
    up_pre = own_ref[1] + got_ref[0, 1].astype(F32)
    for far in far_refs:
        gate_pre += far[0].astype(F32)
        up_pre += far[1].astype(F32)
    sigma_gate = jax.nn.sigmoid(gate_pre)
    upstream = upstream_ref[:, at].astype(F32)
    gated = gate_pre * sigma_gate
    hidden_ref[:, at] = (gated * up_pre).astype(BF16)
    slope = sigma_gate * (1.0 + gate_pre * (1.0 - sigma_gate))
    grads_ref[0] = (upstream * up_pre * slope).astype(BF16)
    grads_ref[1] = (upstream * gated).astype(BF16)


def middle_part(outer, at, own, got, far, hidden_grad, hidden, after):
    rows, width = own.shape[1:]
    first = hidden is None
    args = [own, got, hidden_grad, *far, *after] + ([] if first else [hidden])
    return call(
        functools.partial(middle_kernel, outer, at, first, len(after)),
        "middle_part",
        [WHOLE] * (2 + outer) + [REMOTE] * len(after) + [WHOLE] * (not first),
        [WHOLE] * 2,
        [
            jax.ShapeDtypeStruct(hidden_grad.shape, BF16),
            jax.ShapeDtypeStruct((2, rows, width), BF16),
        ],
        [],
        rows * width,
        args,
    )


def input_kernel(quarters, rows, columns, first, last, skipped, gate_ref, up_ref, *refs):
    pieces, rest = refs[:quarters], refs[quarters + skipped :]
    earlier = []
    if not first:
        count = 2 if last else 1
        earlier, rest = rest[:count], rest[count:]
    *sums, grads, weights, sems = rest
    depth, deep = gate_ref.shape[0], weights.shape[2]
    slots = weights.shape[1]
    queue = [
        [
            pltpu.make_async_copy(
                source.at[pl.ds(d * deep, deep), columns],
                weights.at[k, d % slots],
                sems.at[k, d % slots],
            )
            for k, source in enumerate((gate_ref, up_ref))
        ]
        for d in range(depth // deep)
    ]
    for pair in queue[: slots - 1]:
        for copy in pair:
            copy.start()
    outer = quarters // 2
    me = lax.axis_index("row")
    place, core = me // 2, me % 2
    for j, piece in enumerate(pieces):
        step, swap = j // 2, j % 2
        there = (place + outer - step) % outer * 2
        at = pl.multiple_of((there + (core + swap) % 2) * rows, rows)
        for k in range(2):
            grads[k, pl.ds(at, rows), :] = piece[k]
    dims = (((1,), (1,)), ((), ()))
    flipped = [] if last else [grads[k].T for k in range(2)]
    half = depth // 2
    for d, pair in enumerate(queue):
        for copy in pair:
            copy.wait()
        for copy in queue[d + slots - 1] if d + slots - 1 < len(queue) else []:
            copy.start()
        at = slice(d * deep, (d + 1) * deep)
        index, across = d * deep // half, slice(d * deep % half, d * deep % half + deep)
        term = None
        if not first:
            term = earlier[index][:, across] if last else earlier[0][at, :]
        for k in range(2):
            piece = weights[k, d % slots]
            if last:
                product = lax.dot_general(grads[k], piece, dims, preferred_element_type=F32)
            else:
                product = jnp.dot(piece, flipped[k], preferred_element_type=F32)
            term = product if term is None else term + product
        if last:
            sums[index][:, across] = term
        elif len(sums) == 1:
            sums[0][at, :] = term
        else:
            sums[index][:, across] = term.T


def input_part(quarters, block, chunk, gate_weight, up_weight, pieces, acc, final, after):
    depth = gate_weight.shape[0]
    rows = pieces[0].shape[1]
    tokens = rows * quarters
    start, count = chunk
    width = count * block
    deep = 256 if depth % 512 == 0 else 128
    first, last = acc is None, final == 0
    args = [in_hbm(gate_weight), in_hbm(up_weight), *pieces, *after] + ([] if first else acc)
    sums = [jax.ShapeDtypeStruct((depth, tokens), F32)]
    if final <= 1:
        sums = [jax.ShapeDtypeStruct((tokens, depth // 2), F32)] * 2
    columns = pl.ds(start * block, width)
    *acc, grads = call(
        functools.partial(input_kernel, quarters, rows, columns, first, last, len(after)),
        "input_part",
        [REMOTE] * 2
        + [WHOLE] * quarters
        + [REMOTE] * len(after)
        + [WHOLE] * (0 if first else len(acc)),
        [WHOLE] * (len(sums) + 1),
        sums + [jax.ShapeDtypeStruct((2, tokens, width), BF16)],
        [pltpu.VMEM((2, SLOTS, deep, width), BF16), pltpu.SemaphoreType.DMA((2, SLOTS))],
        tokens * depth * width,
        args,
    )
    return acc, grads


def weight_kernel(block, start, count, skipped, xt_ref, grads_ref, *refs):
    gate_out, up_out, products, sems = refs[skipped:]
    xt = xt_ref[...]
    slots = products.shape[0]
    copies = []
    for j in range(count):
        for k, out in enumerate((gate_out, up_out)):
            piece = grads_ref[k, :, j * block : (j + 1) * block]
            slot = len(copies) % slots
            if len(copies) >= slots:
                copies[-slots].wait()
            products[slot] = jnp.dot(xt, piece, preferred_element_type=F32).astype(BF16)
            copy = pltpu.make_async_copy(
                products.at[slot], out.at[:, pl.ds((start + j) * block, block)], sems.at[slot]
            )
            copy.start()
            copies.append(copy)
    for copy in copies[-slots:]:
        copy.wait()


def weight_part(block, start, count, full, xt, grads, state, after):
    depth, tokens = xt.shape
    args = [xt, grads, *after, *[in_hbm(value) for value in state]]
    first = 2 + len(after)
    aliases = {first + k: k for k in range(len(state))}
    return call(
        functools.partial(weight_kernel, block, start, count, len(args) - 2),
        "weight_part",
        [WHOLE] * 2 + [REMOTE] * (len(args) - 2),
        [REMOTE] * 2,
        [pltpu.HBM((depth, full), BF16)] * 2,
        [pltpu.VMEM((SLOTS, depth, block), BF16), pltpu.SemaphoreType.DMA((SLOTS,))],
        tokens * depth * count * block,
        args,
        aliases,
    )


def token_sums(halves, columns, orders):
    position = lax.axis_index("col")
    bits = len(orders[0])
    rows = halves[0].shape[0] // columns
    halves = [half.reshape((2,) * bits + (rows, half.shape[1])) for half in halves]
    lefts = [list(reversed(range(bits))) for _ in halves]
    stages = []
    for stage in range(bits):
        kept, got = [], []
        for half, left, order in zip(halves, lefts, orders):
            bit = order[stage]
            axis = left.index(bit)
            left.remove(bit)
            mine = (position // 2**bit) % 2
            send = lax.dynamic_index_in_dim(half, 1 - mine, axis, keepdims=False)
            moves = [(c, c ^ 2**bit) for c in range(columns)]
            got.append(lax.ppermute(send.astype(BF16), "col", moves))
            kept.append(lax.dynamic_index_in_dim(half, mine, axis, keepdims=False))
        halves = [keep + far.astype(F32) for keep, far in zip(kept, got)]
        stages.append(halves)
    return stages


def local(quarters, columns, inputs, gate_weight, up_weight, hidden_grad):
    outer = quarters // 2
    full = gate_weight.shape[1]
    block, chunks = chunk_list(full)
    swap = [(r, r ^ 1) for r in range(quarters)]

    def sibling(value):
        return lax.ppermute(value, "row", swap)

    def across(value, step):
        moves = [(r, (r // 2 + step) % outer * 2 + r % 2) for r in range(quarters)]
        return lax.ppermute(value, "row", moves)

    def forward(i, x, early, after):
        following = chunks[i + 1][0] if i + 1 < len(chunks) else None
        own, far, send, *loaded = forward_part(
            quarters, block, chunks[i], following, x, gate_weight, up_weight, early, after
        )
        if i == 0:
            x, loaded = loaded[0], loaded[1:]
        got = sibling(send)
        near = [(far[step - 1] + got[step].astype(F32)).astype(BF16) for step in range(1, outer)]
        owns.append(own)
        gots.append(got)
        sums.append(near)
        crossed.append([across(value, step + 1) for step, value in enumerate(near)])
        return x, loaded

    def middle(i, hidden, after):
        start, count = chunks[i]
        at = slice(start * block, (start + count) * block)
        hidden, mine = middle_part(
            outer, at, owns[i], gots[i], crossed[i], hidden_grad, hidden, after
        )
        group = [mine, sibling(mine)]
        for step in range(1, outer):
            there = across(mine, step)
            group += [there, sibling(there)]
        pieces.append(group)
        return hidden

    owns, gots, sums, crossed, pieces = [], [], [], [], []
    number = len(chunks)
    x, early, hidden = inputs, [], None
    for i in range(number):
        after = []
        if i >= 2:
            after = sums[i - 2][:1]
        if i >= 3:
            hidden = middle(i - 3, hidden, [])
            after = after + [pieces[i - 3][0]]
        x, early = forward(i, x, early, after)
    for i in range(max(number - 3, 0), number):
        hidden = middle(i, hidden, pieces[i - 2][2:3] if i >= 2 else [])

    xt = x.T
    bits = columns.bit_length() - 1
    order = list(range(bits))
    acc, state = None, []
    grads = []
    for i in range(number):
        after = [in_hbm(value) for value in state[:1]] if i == number - 1 else []
        acc, whole = input_part(
            quarters, block, chunks[i], gate_weight, up_weight, pieces[i], acc, number - 1 - i, after
        )
        grads.append(whole)
        if i < number - 2:
            state = weight_part(block, *chunks[i], full, xt, whole, state, [])
    stages = [acc] + token_sums(acc, columns, [order, order[1::-1] + order[2:]])
    input_grad = jnp.concatenate([half.astype(BF16) for half in stages[-1]], axis=1)
    for i in range(max(number - 2, 0), number):
        after = stages[min(i - max(number - 2, 0), bits)]
        state = weight_part(block, *chunks[i], full, xt, grads[i], state, after)
    return hidden, input_grad, state[0], state[1]


def solution(mesh):
    return jax.shard_map(
        functools.partial(local, mesh.shape["row"], mesh.shape["col"]),
        mesh=mesh,
        in_specs=(P(None, "row"), P("row", "col"), P("row", "col"), P("row", "col")),
        out_specs=(P("row", "col"), P("col", "row"), P("row", "col"), P("row", "col")),
        check_vma=False,
    )
```

```python
import functools

import jax
import jax.numpy as jnp
from jax import lax
from jax.experimental import pallas as pl
from jax.experimental.pallas import tpu as pltpu
from jax.sharding import PartitionSpec as P

BF16 = jnp.bfloat16
F32 = jnp.float32
VMEM_BYTES = 24 * 1024 * 1024
SHARES = (2, 4, 5, 3)
SLOTS = 4
COST = 40
WHOLE = pl.BlockSpec(memory_space=pltpu.VMEM)
REMOTE = pl.BlockSpec(memory_space=pl.ANY)


def chunk_list(width):
    block = 256 if width % 256 == 0 else 128
    units = width // block
    total = sum(SHARES)
    edges = [0]
    run = 0
    for share in SHARES:
        run += share
        edges.append(max(min(units, round(units * run / total)), edges[-1]))
    return block, [(a, b - a) for a, b in zip(edges, edges[1:]) if b > a]


def call(kernel, name, in_specs, out_specs, out_shape, scratch, size, args, aliases=None):
    return pl.pallas_call(
        kernel,
        in_specs=in_specs,
        out_specs=out_specs,
        out_shape=out_shape,
        scratch_shapes=scratch,
        input_output_aliases=aliases or {},
        compiler_params=pltpu.CompilerParams(vmem_limit_bytes=VMEM_BYTES),
        cost_estimate=pl.CostEstimate(
            flops=COST * size, bytes_accessed=size, transcendentals=0
        ),
        name=name,
    )(*args)


def in_hbm(value):
    return pltpu.with_memory_space_constraint(value, pltpu.HBM)


def in_order(value, after):
    return call(
        lambda *refs: None,
        "in_order",
        [REMOTE] * (1 + len(after)),
        REMOTE,
        jax.ShapeDtypeStruct(value.shape, value.dtype),
        [],
        1,
        [value, *after],
        {0: 0},
    )


def forward_kernel(layout, ins, outs, *refs):
    quarters, rows, block, start, count, following, first = layout
    given, made = refs[:ins], refs[ins : ins + outs]
    weights, total, sems, x_sem = refs[ins + outs :]
    sources = given[1:3]
    own_ref, far_ref, send_ref, *made = made
    x_ref, early = given[0], given[3:5]
    if first:
        x_copy = pltpu.make_async_copy(x_ref, made[0], x_sem)
        x_copy.start()
        x_ref, made = made[0], made[1:]
    slots = weights.shape[1]
    queue = [
        [
            pltpu.make_async_copy(
                source.at[:, pl.ds((start + j) * block, block)],
                weights.at[k, j % slots],
                sems.at[k, j % slots],
            )
            for k, source in enumerate(sources)
        ]
        for j in range(0 if first else 1, count)
    ]
    if made:
        queue.append(
            [
                pltpu.make_async_copy(
                    source.at[:, pl.ds(following * block, block)], target, sems.at[k, slots]
                )
                for k, (source, target) in enumerate(zip(sources, made))
            ]
        )
    for pair in queue[: slots - 1]:
        for copy in pair:
            copy.start()
    if first:
        x_copy.wait()
    outer = quarters // 2
    me = lax.axis_index("row")
    place, core = me // 2, me % 2
    x = x_ref[...]
    taken = 0
    for j in range(count):
        at = slice(j * block, (j + 1) * block)
        if first or j:
            for copy in queue[taken]:
                copy.wait()
            taken += 1
            more = taken + slots - 2
            for copy in queue[more] if more < len(queue) else []:
                copy.start()
            blocks = [weights[k, j % slots] for k in range(2)]
        else:
            blocks = [ref[...] for ref in early]
        for k in range(2):
            total[k] = jnp.dot(x, blocks[k], preferred_element_type=F32)
        for step in range(outer):
            there = (place + step) % outer * 2
            mine = pl.multiple_of((there + core) * rows, rows)
            other = pl.multiple_of((there + 1 - core) * rows, rows)
            for k in range(2):
                kept = total[k, pl.ds(mine, rows), :]
                if step == 0:
                    own_ref[k, :, at] = kept
                else:
                    far_ref[step - 1, k, :, at] = kept
                send_ref[step, k, :, at] = total[k, pl.ds(other, rows), :].astype(BF16)
    for pair in queue[taken:]:
        for copy in pair:
            copy.wait()


def forward_part(quarters, block, chunk, following, x, gate_weight, up_weight, early, after):
    tokens, depth = x.shape
    rows = tokens // quarters
    outer = quarters // 2
    start, count = chunk
    width = count * block
    first = not early
    out_shape = [
        jax.ShapeDtypeStruct((2, rows, width), F32),
        jax.ShapeDtypeStruct((outer - 1, 2, rows, width), F32),
        jax.ShapeDtypeStruct((outer, 2, rows, width), BF16),
    ]
    if first:
        x = in_hbm(x)
        out_shape.append(jax.ShapeDtypeStruct(x.shape, BF16))
    if following is not None:
        out_shape += [jax.ShapeDtypeStruct((depth, block), BF16)] * 2
    args = (x, in_hbm(gate_weight), in_hbm(up_weight), *early, *after)
    layout = (quarters, rows, block, start, count, following, first)
    return call(
        functools.partial(forward_kernel, layout, len(args), len(out_shape)),
        "forward_part",
        [REMOTE if first else WHOLE, REMOTE, REMOTE]
        + [WHOLE] * len(early)
        + [REMOTE] * len(after),
        [WHOLE] * len(out_shape),
        out_shape,
        [
            pltpu.VMEM((2, SLOTS, depth, block), BF16),
            pltpu.VMEM((2, tokens, block), F32),
            pltpu.SemaphoreType.DMA((2, SLOTS + 1)),
            pltpu.SemaphoreType.DMA,
        ],
        tokens * depth * width,
        args,
    )


def middle_kernel(outer, at, first, skipped, own_ref, got_ref, upstream_ref, *refs):
    far_refs, rest = refs[: outer - 1], refs[outer - 1 + skipped :]
    if not first:
        rest[1][...] = rest[0][...]
        rest = rest[1:]
    hidden_ref, grads_ref = rest
    gate_pre = own_ref[0] + got_ref[0, 0].astype(F32)
    up_pre = own_ref[1] + got_ref[0, 1].astype(F32)
    for far in far_refs:
        gate_pre += far[0].astype(F32)
        up_pre += far[1].astype(F32)
    sigma_gate = jax.nn.sigmoid(gate_pre)
    upstream = upstream_ref[:, at].astype(F32)
    gated = gate_pre * sigma_gate
    hidden_ref[:, at] = (gated * up_pre).astype(BF16)
    slope = sigma_gate * (1.0 + gate_pre * (1.0 - sigma_gate))
    grads_ref[0] = (upstream * up_pre * slope).astype(BF16)
    grads_ref[1] = (upstream * gated).astype(BF16)


def middle_part(outer, at, own, got, far, hidden_grad, hidden, after):
    rows, width = own.shape[1:]
    first = hidden is None
    args = [own, got, hidden_grad, *far, *after] + ([] if first else [hidden])
    return call(
        functools.partial(middle_kernel, outer, at, first, len(after)),
        "middle_part",
        [WHOLE] * (2 + outer) + [REMOTE] * len(after) + [WHOLE] * (not first),
        [WHOLE] * 2,
        [
            jax.ShapeDtypeStruct(hidden_grad.shape, BF16),
            jax.ShapeDtypeStruct((2, rows, width), BF16),
        ],
        [],
        rows * width,
        args,
    )


def input_kernel(layout, gate_ref, up_ref, *refs):
    quarters, rows, columns, held, first, last, skipped, extra = layout
    refs = refs[skipped:]
    pieces, rest = refs[:quarters], refs[quarters:]
    earlier, rest = rest[:extra], rest[extra:]
    if first:
        x_ref, rest = rest[0], rest[1:]
    depth = gate_ref.shape[0]
    half = depth // 2
    if held:
        *sums, grads = rest
        weights, copies = (gate_ref, up_ref), []
    else:
        *sums, grads, scratch, sems = rest
        weights = (scratch.at[0], scratch.at[1])
        copies = [
            pltpu.make_async_copy(
                source.at[pl.ds(h * half, half), columns],
                scratch.at[k, pl.ds(h * half, half)],
                sems.at[k, h],
            )
            for h in range(2)
            for k, source in enumerate((gate_ref, up_ref))
        ]
        for copy in copies:
            copy.start()
    outer = quarters // 2
    me = lax.axis_index("row")
    place, core = me // 2, me % 2
    for j, piece in enumerate(pieces):
        step, swap = j // 2, j % 2
        there = (place + outer - step) % outer * 2
        at = pl.multiple_of((there + (core + swap) % 2) * rows, rows)
        for k in range(2):
            grads[k, pl.ds(at, rows), :] = piece[k]
    if first:
        xt_ref, sums = sums[0], sums[1:]
        xt_ref[...] = x_ref[...].T
    dims = (((1,), (1,)), ((), ()))
    flipped = [] if last else [grads[k].T for k in range(2)]
    deep = 256 if depth % 512 == 0 else 128
    for d in range(depth // deep):
        at = slice(d * deep, (d + 1) * deep)
        index, across = d * deep // half, slice(d * deep % half, d * deep % half + deep)
        if copies and d * deep % half == 0:
            copies[2 * index].wait()
            copies[2 * index + 1].wait()
        term = None
        if earlier:
            term = earlier[index][:, across] if last else earlier[0][at, :]
        for k in range(2):
            piece = weights[k][at, :]
            if last:
                product = lax.dot_general(grads[k], piece, dims, preferred_element_type=F32)
            else:
                product = jnp.dot(piece, flipped[k], preferred_element_type=F32)
            term = product if term is None else term + product
        if last:
            sums[index][:, across] = term
        elif len(sums) == 1:
            sums[0][at, :] = term
        else:
            sums[index][:, across] = term.T


def input_part(quarters, block, chunk, weights, held, pieces, acc, final, x, after):
    depth = x.shape[1]
    rows = pieces[0].shape[1]
    tokens = rows * quarters
    start, count = chunk
    width = count * block
    first, last = acc is None, final == 0
    args = [*weights, *after, *pieces, *([x] if first else acc)]
    sums = [jax.ShapeDtypeStruct((depth, tokens), F32)]
    if final <= 1:
        sums = [jax.ShapeDtypeStruct((tokens, depth // 2), F32)] * 2
    out_shape = sums + [jax.ShapeDtypeStruct((2, tokens, width), BF16)]
    if first:
        out_shape = [jax.ShapeDtypeStruct((depth, tokens), BF16)] + out_shape
    columns = pl.ds(start * block, width)
    layout = (quarters, rows, columns, held, first, last, len(after), 0 if first else len(acc))
    scratch = []
    if not held:
        scratch = [pltpu.VMEM((2, depth, width), BF16), pltpu.SemaphoreType.DMA((2, 2))]
    out = call(
        functools.partial(input_kernel, layout),
        "input_part",
        [WHOLE if held else REMOTE] * 2
        + [REMOTE] * len(after)
        + [WHOLE] * (len(args) - 2 - len(after)),
        [WHOLE] * len(out_shape),
        out_shape,
        scratch,
        tokens * depth,
        args,
    )
    xt, out = (out[0], out[1:]) if first else (None, out)
    return xt, out[:-1], out[-1]


def weight_kernel(block, chunk, ahead, skipped, xt_ref, grads_ref, *refs):
    start, count = chunk
    refs = refs[skipped:]
    sources, refs = (refs[:2], refs[2:]) if ahead else ((), refs)
    refs = refs[2:] if len(refs) > (8 if ahead else 4) else refs
    gate_out, up_out, *loaded, products, sems = refs
    fetched = []
    if ahead:
        loaded, fetch_sems = loaded[:2], loaded[2]
        half = loaded[0].shape[0] // 2
        fetched = [
            pltpu.make_async_copy(
                source.at[pl.ds(h * half, half), ahead],
                target.at[pl.ds(h * half, half)],
                fetch_sems.at[k, h],
            )
            for h in range(2)
            for k, (source, target) in enumerate(zip(sources, loaded))
        ]
        for copy in fetched:
            copy.start()
    xt = xt_ref[...]
    copies = []
    for j in range(count):
        for k, out in enumerate((gate_out, up_out)):
            piece = grads_ref[k, :, j * block : (j + 1) * block]
            products[k, j] = jnp.dot(xt, piece, preferred_element_type=F32).astype(BF16)
            copy = pltpu.make_async_copy(
                products.at[k, j], out.at[:, pl.ds((start + j) * block, block)], sems.at[k, j]
            )
            copy.start()
            copies.append(copy)
    for copy in fetched + copies:
        copy.wait()


def weight_part(block, chunk, full, xt, grads, state, after, ahead, sources):
    depth, tokens = xt.shape
    start, count = chunk
    columns = pl.ds(ahead[0] * block, ahead[1] * block) if ahead else None
    sources = [in_hbm(value) for value in sources] if ahead else []
    args = [xt, grads, *after, *sources, *[in_hbm(value) for value in state]]
    first = len(args) - len(state)
    aliases = {first + k: k for k in range(len(state))}
    out_shape = [pltpu.HBM((depth, full), BF16)] * 2
    scratch = []
    if ahead:
        out_shape += [jax.ShapeDtypeStruct((depth, ahead[1] * block), BF16)] * 2
        scratch = [pltpu.SemaphoreType.DMA((2, 2))]
    out = call(
        functools.partial(weight_kernel, block, chunk, columns, len(after)),
        "weight_part",
        [WHOLE] * 2 + [REMOTE] * (len(args) - 2),
        [REMOTE] * 2 + [WHOLE] * (len(out_shape) - 2),
        out_shape,
        scratch
        + [pltpu.VMEM((2, count, depth, block), BF16), pltpu.SemaphoreType.DMA((2, count))],
        tokens * depth * count * block,
        args,
        aliases,
    )
    return out[:2], out[2:]


def token_sums(halves, columns, orders):
    position = lax.axis_index("col")
    bits = len(orders[0])
    rows = halves[0].shape[0] // columns
    halves = [half.reshape((2,) * bits + (rows, half.shape[1])) for half in halves]
    lefts = [list(reversed(range(bits))) for _ in halves]
    stages = []
    for stage in range(bits):
        kept, got = [], []
        for half, left, order in zip(halves, lefts, orders):
            bit = order[stage]
            axis = left.index(bit)
            left.remove(bit)
            mine = (position // 2**bit) % 2
            send = lax.dynamic_index_in_dim(half, 1 - mine, axis, keepdims=False)
            moves = [(c, c ^ 2**bit) for c in range(columns)]
            got.append(lax.ppermute(send.astype(BF16), "col", moves))
            kept.append(lax.dynamic_index_in_dim(half, mine, axis, keepdims=False))
        halves = [keep + far.astype(F32) for keep, far in zip(kept, got)]
        stages.append(halves)
    return stages


def local(quarters, columns, inputs, gate_weight, up_weight, hidden_grad):
    outer = quarters // 2
    full = gate_weight.shape[1]
    block, chunks = chunk_list(full)
    swap = [(r, r ^ 1) for r in range(quarters)]

    def sibling(value):
        return lax.ppermute(value, "row", swap)

    def across(value, step):
        moves = [(r, (r // 2 + step) % outer * 2 + r % 2) for r in range(quarters)]
        return lax.ppermute(value, "row", moves)

    number = len(chunks)
    both = [gate_weight, up_weight]
    owns, gots, sums, crossed, pieces, groups, grads = [], [], [], [], [], [], []
    held, flipped = {}, []

    def forward(i, x, early):
        following = chunks[i + 1][0] if i + 1 < number else None
        after = sums[i - 1][:1] if i else []
        own, far, send, *loaded = forward_part(
            quarters, block, chunks[i], following, x, gate_weight, up_weight, early, after
        )
        owns.append(own)
        if i == 0:
            x, loaded = loaded[0], loaded[1:]
        elif i < 3:
            send = in_order(send, crossed[i - 1][:1] + pieces[i - 1][:1])
        else:
            if i == number - 1:
                relay(0, sums[-1][:1])
                take_input(0, x, None, [])
            send = in_order(send, crossed[i - 1][:1] + pieces[i - 3][2:3] + grads)
        got = sibling(send)
        near = [(far[step - 1] + got[step].astype(F32)).astype(BF16) for step in range(1, outer)]
        gots.append(got)
        sums.append(near)
        crossed.append([across(value, step + 1) for step, value in enumerate(near)])
        return x, loaded

    def middle(i, hidden):
        start, count = chunks[i]
        at = slice(start * block, (start + count) * block)
        after = pieces[i - 2][2:3] if i >= 2 else []
        hidden, mine = middle_part(
            outer, at, owns[i], gots[i], crossed[i], hidden_grad, hidden, after
        )
        pieces.append([mine, sibling(mine)] + [across(mine, step) for step in range(1, outer)])
        return hidden

    def relay(i, after):
        mine, near, *far = pieces[i]
        group = [mine, near]
        for there in far:
            group += [there, sibling(in_order(there, after) if after else there)]
        groups.append(group)

    def take_input(i, x, acc, after):
        weights = held[i] if i in held else [in_hbm(value) for value in both]
        xt, total, whole = input_part(
            quarters, block, chunks[i], weights, i in held, groups[i], acc, number - 1 - i, x, after
        )
        if i == 0:
            flipped.append(xt)
            totals.append(total)
        grads.append(whole)
        return total

    totals = []
    x, early, hidden = inputs, [], None
    for i in range(number):
        x, early = forward(i, x, early)
        hidden = middle(i, hidden)
    acc, state = None, []
    for i in range(number):
        if i == 0 and grads:
            acc = totals[0]
        else:
            last = i == number - 1
            relay(i, [] if last else grads[-1:] + pieces[-1][:1] if i == number - 2 else sums[-1][:1])
            after = pieces[i + 1][:1] + sums[-1][:1] if i == 1 < number - 1 else []
            acc = take_input(i, x, acc, after)
        if i < number - 2:
            state, held[i + 2] = weight_part(
                block, chunks[i], full, flipped[0], grads[i], state, [], chunks[i + 2], both
            )
    bits = columns.bit_length() - 1
    order = list(range(bits))
    stages = [acc] + token_sums(acc, columns, [order, order[1::-1] + order[2:]])
    input_grad = jnp.concatenate([half.astype(BF16) for half in stages[-1]], axis=1)
    for i in range(max(number - 2, 0), number):
        after = stages[min(i - max(number - 2, 0), bits)]
        state, _ = weight_part(
            block, chunks[i], full, flipped[0], grads[i], state, after, None, []
        )
    return hidden, input_grad, state[0], state[1]


def solution(mesh):
    return jax.shard_map(
        functools.partial(local, mesh.shape["row"], mesh.shape["col"]),
        mesh=mesh,
        in_specs=(P(None, "row"), P("row", "col"), P("row", "col"), P("row", "col")),
        out_specs=(P("row", "col"), P("col", "row"), P("row", "col"), P("row", "col")),
        check_vma=False,
    )
```

```python
import functools
import math

import jax
import jax.numpy as jnp
from jax import lax
from jax.experimental import pallas as pl
from jax.experimental.pallas import tpu as pltpu
from jax.sharding import PartitionSpec as P

BF16 = jnp.bfloat16
F32 = jnp.float32
VMEM_BYTES = 6 * 1024 * 1024
SHARES = (2, 4, 5, 3)
SLOTS = 3
COST = 40
WHOLE = pl.BlockSpec(memory_space=pltpu.VMEM)
REMOTE = pl.BlockSpec(memory_space=pl.ANY)


def chunk_list(width):
    block = 256 if width % 256 == 0 else 128
    units = width // block
    total = sum(SHARES)
    edges = [0]
    run = 0
    for share in SHARES:
        run += share
        edges.append(max(min(units, round(units * run / total)), edges[-1]))
    return block, [(a, b - a) for a, b in zip(edges, edges[1:]) if b > a]


def call(kernel, name, in_specs, out_specs, out_shape, scratch, size, args, aliases=None, room=0):
    held = [item for item in scratch if len(getattr(item, 'shape', ())) > 2]
    room += VMEM_BYTES + sum(math.prod(item.shape) * item.dtype.itemsize for item in held)
    return pl.pallas_call(
        kernel,
        in_specs=in_specs,
        out_specs=out_specs,
        out_shape=out_shape,
        scratch_shapes=scratch,
        input_output_aliases=aliases or {},
        compiler_params=pltpu.CompilerParams(vmem_limit_bytes=room),
        cost_estimate=pl.CostEstimate(
            flops=COST * size, bytes_accessed=size, transcendentals=0
        ),
        name=name,
    )(*args)


def in_hbm(value):
    return pltpu.with_memory_space_constraint(value, pltpu.HBM)


def in_order(value, after):
    return call(
        lambda *refs: None,
        "in_order",
        [REMOTE] * (1 + len(after)),
        REMOTE,
        jax.ShapeDtypeStruct(value.shape, value.dtype),
        [],
        1,
        [value, *after],
        {0: 0},
    )


def pack_kernel(count, *refs):
    for step, ref in enumerate(refs[:count]):
        refs[-1][step] = ref[...]


def packed(values, after):
    return call(
        functools.partial(pack_kernel, len(values)),
        "packed",
        [WHOLE] * len(values) + [REMOTE] * len(after),
        WHOLE,
        jax.ShapeDtypeStruct((len(values), *values[0].shape), values[0].dtype),
        [],
        1,
        [*values, *after],
    )


def forward_kernel(layout, ins, outs, *refs):
    quarters, rows, block, start, count, following, first = layout
    given, made = refs[:ins], refs[ins : ins + outs]
    weights, total, sems, x_sem = refs[ins + outs :]
    sources = given[1:3]
    own_ref, far_ref, send_ref, *made = made
    x_ref, early = given[0], given[3:5]
    if first:
        x_copy = pltpu.make_async_copy(x_ref, made[0], x_sem)
        x_copy.start()
        x_ref, made = made[0], made[1:]
    slots = weights.shape[1]
    queue = [
        [
            pltpu.make_async_copy(
                source.at[:, pl.ds((start + j) * block, block)],
                weights.at[k, j % slots],
                sems.at[k, j % slots],
            )
            for k, source in enumerate(sources)
        ]
        for j in range(0 if first else 1, count)
    ]
    if made:
        queue.append(
            [
                pltpu.make_async_copy(
                    source.at[:, pl.ds(following * block, block)], target, sems.at[k, slots]
                )
                for k, (source, target) in enumerate(zip(sources, made))
            ]
        )
    for pair in queue[: slots - 1]:
        for copy in pair:
            copy.start()
    if first:
        x_copy.wait()
    outer = quarters // 2
    me = lax.axis_index("row")
    place, core = me // 2, me % 2
    x = x_ref[...]
    taken = 0
    for j in range(count):
        at = slice(j * block, (j + 1) * block)
        if first or j:
            for copy in queue[taken]:
                copy.wait()
            taken += 1
            more = taken + slots - 2
            for copy in queue[more] if more < len(queue) else []:
                copy.start()
            blocks = [weights[k, j % slots] for k in range(2)]
        else:
            blocks = [ref[...] for ref in early]
        for k in range(2):
            total[k] = jnp.dot(x, blocks[k], preferred_element_type=F32)
        for step in range(outer):
            there = (place + step) % outer * 2
            mine = pl.multiple_of((there + core) * rows, rows)
            other = pl.multiple_of((there + 1 - core) * rows, rows)
            for k in range(2):
                kept = total[k, pl.ds(mine, rows), :]
                if step == 0:
                    own_ref[k, :, at] = kept
                else:
                    far_ref[step - 1, k, :, at] = kept
                send_ref[step, k, :, at] = total[k, pl.ds(other, rows), :].astype(BF16)
    for pair in queue[taken:]:
        for copy in pair:
            copy.wait()


def forward_part(quarters, block, chunk, following, x, gate_weight, up_weight, early, after):
    tokens, depth = x.shape
    rows = tokens // quarters
    outer = quarters // 2
    start, count = chunk
    width = count * block
    first = not early
    out_shape = [
        jax.ShapeDtypeStruct((2, rows, width), F32),
        jax.ShapeDtypeStruct((outer - 1, 2, rows, width), F32),
        jax.ShapeDtypeStruct((outer, 2, rows, width), BF16),
    ]
    if first:
        x = in_hbm(x)
        out_shape.append(jax.ShapeDtypeStruct(x.shape, BF16))
    if following is not None:
        out_shape += [jax.ShapeDtypeStruct((depth, block), BF16)] * 2
    args = (x, in_hbm(gate_weight), in_hbm(up_weight), *early, *after)
    layout = (quarters, rows, block, start, count, following, first)
    return call(
        functools.partial(forward_kernel, layout, len(args), len(out_shape)),
        "forward_part",
        [REMOTE if first else WHOLE, REMOTE, REMOTE]
        + [WHOLE] * len(early)
        + [REMOTE] * len(after),
        [WHOLE] * len(out_shape),
        out_shape,
        [
            pltpu.VMEM((2, SLOTS, depth, block), BF16),
            pltpu.VMEM((2, tokens, block), F32),
            pltpu.SemaphoreType.DMA((2, SLOTS + 1)),
            pltpu.SemaphoreType.DMA,
        ],
        tokens * depth * width,
        args,
    )


def middle_kernel(outer, at, first, skipped, own_ref, got_ref, upstream_ref, *refs):
    far_refs, rest = refs[: outer - 1], refs[outer - 1 + skipped :]
    if not first:
        rest[1][...] = rest[0][...]
        rest = rest[1:]
    hidden_ref, grads_ref = rest
    gate_pre = own_ref[0] + got_ref[0, 0].astype(F32)
    up_pre = own_ref[1] + got_ref[0, 1].astype(F32)
    for far in far_refs:
        gate_pre += far[0].astype(F32)
        up_pre += far[1].astype(F32)
    sigma_gate = jax.nn.sigmoid(gate_pre)
    upstream = upstream_ref[:, at].astype(F32)
    gated = gate_pre * sigma_gate
    hidden_ref[:, at] = (gated * up_pre).astype(BF16)
    slope = sigma_gate * (1.0 + gate_pre * (1.0 - sigma_gate))
    grads_ref[0] = (upstream * up_pre * slope).astype(BF16)
    grads_ref[1] = (upstream * gated).astype(BF16)


def middle_part(outer, at, own, got, far, hidden_grad, hidden, after):
    rows, width = own.shape[1:]
    first = hidden is None
    args = [own, got, hidden_grad, *far, *after] + ([] if first else [hidden])
    return call(
        functools.partial(middle_kernel, outer, at, first, len(after)),
        "middle_part",
        [WHOLE] * (2 + outer) + [REMOTE] * len(after) + [WHOLE] * (not first),
        [WHOLE] * 2,
        [
            jax.ShapeDtypeStruct(hidden_grad.shape, BF16),
            jax.ShapeDtypeStruct((2, rows, width), BF16),
        ],
        [],
        rows * width,
        args,
    )


def input_kernel(layout, ins, outs, *refs):
    quarters, rows, block, chunk, held, first, last, skipped, write, old, ahead = layout
    given, made, scratch = refs[:ins], list(refs[ins : ins + outs]), list(refs[ins + outs :])
    (gate_ref, up_ref), given = given[:2], given[2 + skipped :]
    outer = quarters // 2
    pieces, given = given[: outer + 1], list(given[outer + 1 :])
    sources = (gate_ref, up_ref)
    depth = gate_ref.shape[0]
    half = depth // 2
    earlier = []
    if first:
        x_ref, xt_ref = given.pop(0), made.pop(0)
    else:
        earlier = [given.pop(0) for _ in range(old)]
    if write and not first:
        xt_ref = given.pop(0)
    if ahead and held:
        sources = (given.pop(0), given.pop(0))
    loaded = [made.pop() for _ in range(2)][::-1] if ahead else []
    grad_outs = [made.pop() for _ in range(2)][::-1] if write else []
    grads = made.pop()
    sums = made

    def fetch(columns, targets, sems):
        return [
            pltpu.make_async_copy(
                source.at[pl.ds(h * half, half), columns],
                target.at[pl.ds(h * half, half)],
                sems.at[k, h],
            )
            for h in range(2)
            for k, (source, target) in enumerate(zip(sources, targets))
        ]

    weights, copies, later, writes = (gate_ref, up_ref), [], [], []
    start, count = chunk
    if not held:
        store, sems = scratch.pop(0), scratch.pop(0)
        weights = (store.at[0], store.at[1])
        copies = fetch(pl.ds(start * block, count * block), weights, sems)
        for copy in copies:
            copy.start()
    if ahead:
        later = fetch(pl.ds(ahead[0] * block, ahead[1] * block), loaded, scratch.pop())
    if held:
        for copy in later:
            copy.start()
    me = lax.axis_index("row")
    place, core = me // 2, me % 2
    for step in range(outer):
        there = (place + outer - step) % outer * 2
        mine = pl.multiple_of((there + core) * rows, rows)
        other = pl.multiple_of((there + 1 - core) * rows, rows)
        for k in range(2):
            grads[k, pl.ds(mine, rows), :] = pieces[step][k]
            grads[k, pl.ds(other, rows), :] = pieces[outer][step, k]
    if first:
        xt_ref[...] = x_ref[...].T
    if write:
        products, sems = scratch
        writes = weight_terms(block, chunk, xt_ref, grads, grad_outs, products, sems)
    dims = (((1,), (1,)), ((), ()))
    flipped = [] if last else [grads[k].T for k in range(2)]
    deep = 256 if depth % 512 == 0 else 128
    for d in range(depth // deep):
        at = slice(d * deep, (d + 1) * deep)
        index, across = d * deep // half, slice(d * deep % half, d * deep % half + deep)
        if copies and d * deep % half == 0:
            copies[2 * index].wait()
            copies[2 * index + 1].wait()
            for copy in later[2 * index : 2 * index + 2]:
                copy.start()
        term = None
        if earlier:
            term = earlier[index][:, across] if last else earlier[0][at, :]
        for k in range(2):
            piece = weights[k][at, :]
            if last:
                product = lax.dot_general(grads[k], piece, dims, preferred_element_type=F32)
            else:
                product = jnp.dot(piece, flipped[k], preferred_element_type=F32)
            term = product if term is None else term + product
        if last:
            sums[index][:, across] = term
        elif len(sums) == 1:
            sums[0][at, :] = term
        else:
            sums[index][:, across] = term.T
    for copy in writes + later:
        copy.wait()


def input_part(quarters, block, chunk, weights, held, pieces, acc, final, x, after, write, ahead):
    depth, tokens = x.shape[1], x.shape[0]
    rows = tokens // quarters
    start, count = chunk
    width = count * block
    first, last = acc is None, final == 0
    args = [*weights, *after, *pieces, *([x] if first else acc)]
    in_specs = [WHOLE if held else REMOTE] * 2 + [REMOTE] * len(after)
    in_specs += [WHOLE] * (len(args) - len(in_specs))
    out_shape = [jax.ShapeDtypeStruct((depth, tokens), BF16)] if first else []
    out_shape += [jax.ShapeDtypeStruct((tokens, depth // 2), F32)] * 2 if final <= 1 else [
        jax.ShapeDtypeStruct((depth, tokens), F32)
    ]
    out_shape.append(jax.ShapeDtypeStruct((2, tokens, width), BF16))
    scratch, aliases, room = [], {}, 0
    if not held:
        scratch += [pltpu.VMEM((2, depth, width), BF16), pltpu.SemaphoreType.DMA((2, 2))]
    out_specs = [WHOLE] * len(out_shape)
    if write:
        xt, state, full = write
        args += [] if first else [xt]
        in_specs += [] if first else [WHOLE]
    if ahead:
        (chunk_ahead, sources), ahead = ahead, ahead[0]
        if held:
            args += [in_hbm(value) for value in sources]
            in_specs += [REMOTE] * 2
    if write:
        aliases = {len(args) + k: len(out_shape) + k for k in range(len(state))}
        args += [in_hbm(value) for value in state]
        in_specs += [REMOTE] * len(state)
        out_shape += [pltpu.HBM((depth, full), BF16)] * 2
        out_specs += [REMOTE] * 2
        scratch += [pltpu.VMEM((2, count, depth, block), BF16), pltpu.SemaphoreType.DMA((2, count))]
    if ahead:
        out_shape += [jax.ShapeDtypeStruct((depth, ahead[1] * block), BF16)] * 2
        out_specs += [WHOLE] * 2
        scratch.append(pltpu.SemaphoreType.DMA((2, 2)))
    if held or ahead:
        room = 4 * depth * max(width, ahead[1] * block if ahead else 0)
    old = 0 if first else len(acc)
    layout = (quarters, rows, block, chunk, held, first, last, len(after), bool(write), old, ahead)
    out = call(
        functools.partial(input_kernel, layout, len(args), len(out_shape)),
        "input_part",
        in_specs,
        out_specs,
        out_shape,
        scratch,
        tokens * depth * (1 if first else width),
        args,
        aliases,
        room,
    )
    out = list(out)
    xt = out.pop(0) if first else None
    fetched = [out.pop() for _ in range(2)][::-1] if ahead else None
    state = [out.pop() for _ in range(2)][::-1] if write else None
    return xt, out[:-1], out[-1], state, fetched


def weight_terms(block, chunk, xt_ref, grads_ref, outs, products, sems):
    start, count = chunk
    xt = xt_ref[...]
    copies = []
    for j in range(count):
        for k, out in enumerate(outs):
            piece = grads_ref[k, :, j * block : (j + 1) * block]
            products[k, j] = jnp.dot(xt, piece, preferred_element_type=F32).astype(BF16)
            copy = pltpu.make_async_copy(
                products.at[k, j], out.at[:, pl.ds((start + j) * block, block)], sems.at[k, j]
            )
            copy.start()
            copies.append(copy)
    return copies


def weight_kernel(block, chunk, skipped, xt_ref, grads_ref, *refs):
    *outs, products, sems = refs[skipped:]
    for copy in weight_terms(block, chunk, xt_ref, grads_ref, outs, products, sems):
        copy.wait()


def weight_part(block, chunk, full, xt, grads, state, after):
    depth, tokens = xt.shape
    count = chunk[1]
    args = [xt, grads, *after, *[in_hbm(value) for value in state]]
    first = len(args) - len(state)
    return call(
        functools.partial(weight_kernel, block, chunk, len(args) - 2),
        "weight_part",
        [WHOLE] * 2 + [REMOTE] * (len(args) - 2),
        [REMOTE] * 2,
        [pltpu.HBM((depth, full), BF16)] * 2,
        [pltpu.VMEM((2, count, depth, block), BF16), pltpu.SemaphoreType.DMA((2, count))],
        tokens * depth * count * block,
        args,
        {first + k: k for k in range(len(state))},
    )


def token_sums(halves, columns, orders):
    position = lax.axis_index("col")
    bits = len(orders[0])
    rows = halves[0].shape[0] // columns
    halves = [half.reshape((2,) * bits + (rows, half.shape[1])) for half in halves]
    lefts = [list(reversed(range(bits))) for _ in halves]
    stages = []
    for stage in range(bits):
        kept, got = [], []
        for half, left, order in zip(halves, lefts, orders):
            bit = order[stage]
            axis = left.index(bit)
            left.remove(bit)
            mine = (position // 2**bit) % 2
            send = lax.dynamic_index_in_dim(half, 1 - mine, axis, keepdims=False)
            moves = [(c, c ^ 2**bit) for c in range(columns)]
            got.append(lax.ppermute(send.astype(BF16), "col", moves))
            kept.append(lax.dynamic_index_in_dim(half, mine, axis, keepdims=False))
        halves = [keep + far.astype(F32) for keep, far in zip(kept, got)]
        stages.append(halves)
    return stages


def local(quarters, columns, inputs, gate_weight, up_weight, hidden_grad):
    outer = quarters // 2
    full = gate_weight.shape[1]
    block, chunks = chunk_list(full)
    swap = [(r, r ^ 1) for r in range(quarters)]

    def sibling(value):
        return lax.ppermute(value, "row", swap)

    def across(value, step):
        moves = [(r, (r // 2 + step) % outer * 2 + r % 2) for r in range(quarters)]
        return lax.ppermute(value, "row", moves)

    number = len(chunks)
    both = [gate_weight, up_weight]
    owns, gots, sums, crossed, pieces, groups, grads = [], [], [], [], [], [], []
    held, flipped = {}, []

    def forward(i, x, early):
        following = chunks[i + 1][0] if i + 1 < number else None
        after = sums[i - 1][:1] if i else []
        own, far, send, *loaded = forward_part(
            quarters, block, chunks[i], following, x, gate_weight, up_weight, early, after
        )
        owns.append(own)
        if i == 0:
            x, loaded = loaded[0], loaded[1:]
        elif i < 3:
            send = in_order(send, crossed[i - 1][:1] + pieces[i - 1][:1])
        else:
            if i == number - 1:
                relay(0, sums[-1][:1])
                take_input(0, x, None, [])
            send = in_order(send, crossed[i - 1][:1] + pieces[i - 1][:1] + pieces[i - 2][1:2] + grads)
        got = sibling(send)
        near = [(far[step - 1] + got[step].astype(F32)).astype(BF16) for step in range(1, outer)]
        gots.append(got)
        sums.append(near)
        crossed.append([across(value, step + 1) for step, value in enumerate(near)])
        return x, loaded

    def middle(i, hidden, after):
        start, count = chunks[i]
        at = slice(start * block, (start + count) * block)
        hidden, mine = middle_part(
            outer, at, owns[i], gots[i], crossed[i], hidden_grad, hidden, after
        )
        pieces.append([mine] + [across(mine, step) for step in range(1, outer)])
        return hidden

    def relay(i, after):
        groups.append(pieces[i] + [sibling(packed(pieces[i], after))])

    def take_input(i, x, acc, after):
        weights = held[i] if i in held else [in_hbm(value) for value in both]
        write = (flipped[0] if i else None, state, full) if i < number - 2 else None
        later = 2 if i == 0 else 1
        ahead = None
        if later < number - i and i + later not in held and i != 1:
            ahead = (chunks[i + later], both)
        xt, total, whole, written, fetched = input_part(
            quarters, block, chunks[i], weights, i in held, groups[i], acc, number - 1 - i, x,
            after, write, ahead,
        )
        if i == 0:
            flipped.append(xt)
            totals.append(total)
        if written:
            state[:] = written
        if fetched:
            held[i + later] = fetched
        grads.append(whole)
        return total

    totals, state = [], []
    x, early, hidden = inputs, [], None
    for i in range(number):
        x, early = forward(i, x, early)
        if i < 3:
            hidden = middle(i, hidden, pieces[0][1:2] if i == 2 else [])
    acc = None
    for i in range(number):
        if i == 0 and grads:
            acc = totals[0]
            continue
        after = sums[-1][:1] + pieces[i + 1][:1] if i == 1 and number > 3 else []
        relay(i, grads[-1:] + pieces[-1][:1] if i > 1 else sums[-1][:1])
        acc = take_input(i, x, acc, after)
        for j in range(len(pieces), number if i else 0):
            hidden = middle(j, hidden, grads[-1:])
    bits = columns.bit_length() - 1
    order = list(range(bits))
    stages = [acc] + token_sums(acc, columns, [order, order[1::-1] + order[2:]])
    input_grad = jnp.concatenate([half.astype(BF16) for half in stages[-1]], axis=1)
    for i in range(max(number - 2, 0), number):
        after = stages[min(i - max(number - 2, 0), bits)]
        state = weight_part(block, chunks[i], full, flipped[0], grads[i], state, after)
    return hidden, input_grad, state[0], state[1]


def solution(mesh):
    return jax.shard_map(
        functools.partial(local, mesh.shape["row"], mesh.shape["col"]),
        mesh=mesh,
        in_specs=(P(None, "row"), P("row", "col"), P("row", "col"), P("row", "col")),
        out_specs=(P("row", "col"), P("col", "row"), P("row", "col"), P("row", "col")),
        check_vma=False,
    )
```

```python
import functools
import math

import jax
import jax.numpy as jnp
from jax import lax
from jax.experimental import pallas as pl
from jax.experimental.pallas import tpu as pltpu
from jax.sharding import PartitionSpec as P

BF16 = jnp.bfloat16
F32 = jnp.float32
VMEM_BYTES = 6 * 1024 * 1024
SHARES = (3, 6, 5)
SLOTS = 3
COST = 40
WHOLE = pl.BlockSpec(memory_space=pltpu.VMEM)
REMOTE = pl.BlockSpec(memory_space=pl.ANY)


def chunk_list(width):
    block = 256 if width % 256 == 0 else 128
    units = width // block
    total = sum(SHARES)
    edges = [0]
    run = 0
    for share in SHARES:
        run += share
        edges.append(max(min(units, round(units * run / total)), edges[-1]))
    return block, [(a, b - a) for a, b in zip(edges, edges[1:]) if b > a]


def call(kernel, name, in_specs, out_specs, out_shape, scratch, size, args, aliases=None, room=0):
    held = [item for item in scratch if len(getattr(item, 'shape', ())) > 2]
    room += VMEM_BYTES + sum(math.prod(item.shape) * item.dtype.itemsize for item in held)
    return pl.pallas_call(
        kernel,
        in_specs=in_specs,
        out_specs=out_specs,
        out_shape=out_shape,
        scratch_shapes=scratch,
        input_output_aliases=aliases or {},
        compiler_params=pltpu.CompilerParams(vmem_limit_bytes=room),
        cost_estimate=pl.CostEstimate(
            flops=COST * size, bytes_accessed=size, transcendentals=0
        ),
        name=name,
    )(*args)


def in_hbm(value):
    return pltpu.with_memory_space_constraint(value, pltpu.HBM)


def in_order(value, after):
    return call(
        lambda *refs: None,
        "in_order",
        [REMOTE] * (1 + len(after)),
        REMOTE,
        jax.ShapeDtypeStruct(value.shape, value.dtype),
        [],
        1,
        [value, *after],
        {0: 0},
    )


def pack_kernel(count, *refs):
    for step, ref in enumerate(refs[:count]):
        refs[-1][step] = ref[...]


def packed(values, after):
    return call(
        functools.partial(pack_kernel, len(values)),
        "packed",
        [WHOLE] * len(values) + [REMOTE] * len(after),
        WHOLE,
        jax.ShapeDtypeStruct((len(values), *values[0].shape), values[0].dtype),
        [],
        1,
        [*values, *after],
    )


def forward_kernel(layout, ins, outs, *refs):
    quarters, rows, block, start, count, following, first = layout
    given, made = refs[:ins], refs[ins : ins + outs]
    weights, total, sems, x_sem = refs[ins + outs :]
    sources = given[1:3]
    own_ref, far_ref, send_ref, *made = made
    x_ref, early = given[0], given[3:5]
    if first:
        x_copy = pltpu.make_async_copy(x_ref, made[0], x_sem)
        x_copy.start()
        x_ref, made = made[0], made[1:]
    slots = weights.shape[1]
    queue = [
        [
            pltpu.make_async_copy(
                source.at[:, pl.ds((start + j) * block, block)],
                weights.at[k, j % slots],
                sems.at[k, j % slots],
            )
            for k, source in enumerate(sources)
        ]
        for j in range(0 if first else 1, count)
    ]
    if made:
        queue.append(
            [
                pltpu.make_async_copy(
                    source.at[:, pl.ds(following * block, block)], target, sems.at[k, slots]
                )
                for k, (source, target) in enumerate(zip(sources, made))
            ]
        )
    for pair in queue[: slots - 1]:
        for copy in pair:
            copy.start()
    if first:
        x_copy.wait()
    outer = quarters // 2
    me = lax.axis_index("row")
    place, core = me // 2, me % 2
    x = x_ref[...]
    taken = 0
    for j in range(count):
        at = slice(j * block, (j + 1) * block)
        if first or j:
            for copy in queue[taken]:
                copy.wait()
            taken += 1
            more = taken + slots - 2
            for copy in queue[more] if more < len(queue) else []:
                copy.start()
            blocks = [weights[k, j % slots] for k in range(2)]
        else:
            blocks = [ref[...] for ref in early]
        for k in range(2):
            total[k] = jnp.dot(x, blocks[k], preferred_element_type=F32)
        for step in range(outer):
            there = (place + step) % outer * 2
            mine = pl.multiple_of((there + core) * rows, rows)
            other = pl.multiple_of((there + 1 - core) * rows, rows)
            for k in range(2):
                kept = total[k, pl.ds(mine, rows), :]
                if step == 0:
                    own_ref[k, :, at] = kept
                else:
                    far_ref[step - 1, k, :, at] = kept
                send_ref[step, k, :, at] = total[k, pl.ds(other, rows), :].astype(BF16)
    for pair in queue[taken:]:
        for copy in pair:
            copy.wait()


def forward_part(quarters, block, chunk, following, x, gate_weight, up_weight, early, after):
    tokens, depth = x.shape
    rows = tokens // quarters
    outer = quarters // 2
    start, count = chunk
    width = count * block
    first = not early
    out_shape = [
        jax.ShapeDtypeStruct((2, rows, width), F32),
        jax.ShapeDtypeStruct((outer - 1, 2, rows, width), F32),
        jax.ShapeDtypeStruct((outer, 2, rows, width), BF16),
    ]
    if first:
        x = in_hbm(x)
        out_shape.append(jax.ShapeDtypeStruct(x.shape, BF16))
    if following is not None:
        out_shape += [jax.ShapeDtypeStruct((depth, block), BF16)] * 2
    args = (x, in_hbm(gate_weight), in_hbm(up_weight), *early, *after)
    layout = (quarters, rows, block, start, count, following, first)
    return call(
        functools.partial(forward_kernel, layout, len(args), len(out_shape)),
        "forward_part",
        [REMOTE if first else WHOLE, REMOTE, REMOTE]
        + [WHOLE] * len(early)
        + [REMOTE] * len(after),
        [WHOLE] * len(out_shape),
        out_shape,
        [
            pltpu.VMEM((2, SLOTS, depth, block), BF16),
            pltpu.VMEM((2, tokens, block), F32),
            pltpu.SemaphoreType.DMA((2, SLOTS + 1)),
            pltpu.SemaphoreType.DMA,
        ],
        tokens * depth * width,
        args,
    )


def middle_kernel(outer, at, first, skipped, own_ref, got_ref, upstream_ref, *refs):
    far_refs, rest = refs[: outer - 1], refs[outer - 1 + skipped :]
    if not first:
        rest[1][...] = rest[0][...]
        rest = rest[1:]
    hidden_ref, grads_ref = rest
    gate_pre = own_ref[0] + got_ref[0, 0].astype(F32)
    up_pre = own_ref[1] + got_ref[0, 1].astype(F32)
    for far in far_refs:
        gate_pre += far[0].astype(F32)
        up_pre += far[1].astype(F32)
    sigma_gate = jax.nn.sigmoid(gate_pre)
    upstream = upstream_ref[:, at].astype(F32)
    gated = gate_pre * sigma_gate
    hidden_ref[:, at] = (gated * up_pre).astype(BF16)
    slope = sigma_gate * (1.0 + gate_pre * (1.0 - sigma_gate))
    grads_ref[0] = (upstream * up_pre * slope).astype(BF16)
    grads_ref[1] = (upstream * gated).astype(BF16)


def middle_part(outer, at, own, got, far, hidden_grad, hidden, after):
    rows, width = own.shape[1:]
    first = hidden is None
    args = [own, got, hidden_grad, *far, *after] + ([] if first else [hidden])
    return call(
        functools.partial(middle_kernel, outer, at, first, len(after)),
        "middle_part",
        [WHOLE] * (2 + outer) + [REMOTE] * len(after) + [WHOLE] * (not first),
        [WHOLE] * 2,
        [
            jax.ShapeDtypeStruct(hidden_grad.shape, BF16),
            jax.ShapeDtypeStruct((2, rows, width), BF16),
        ],
        [],
        rows * width,
        args,
    )


def input_kernel(layout, ins, outs, *refs):
    quarters, rows, block, chunk, held, first, last, skipped, write, old, ahead = layout
    given, made, scratch = refs[:ins], list(refs[ins : ins + outs]), list(refs[ins + outs :])
    (gate_ref, up_ref), given = given[:2], given[2 + skipped :]
    outer = quarters // 2
    pieces, given = given[: outer + 1], list(given[outer + 1 :])
    sources = (gate_ref, up_ref)
    depth = gate_ref.shape[0]
    half = depth // 2
    earlier = []
    if first:
        x_ref, xt_ref = given.pop(0), made.pop(0)
    else:
        earlier = [given.pop(0) for _ in range(old)]
    if write and not first:
        xt_ref = given.pop(0)
    if ahead and held:
        sources = (given.pop(0), given.pop(0))
    loaded = [made.pop() for _ in range(2)][::-1] if ahead else []
    grad_outs = [made.pop() for _ in range(2)][::-1] if write else []
    grads = made.pop()
    sums = made

    def fetch(columns, targets, sems):
        return [
            pltpu.make_async_copy(
                source.at[pl.ds(h * half, half), columns],
                target.at[pl.ds(h * half, half)],
                sems.at[k, h],
            )
            for h in range(2)
            for k, (source, target) in enumerate(zip(sources, targets))
        ]

    weights, copies, later, writes = (gate_ref, up_ref), [], [], []
    start, count = chunk
    if not held:
        store, sems = scratch.pop(0), scratch.pop(0)
        weights = (store.at[0], store.at[1])
        copies = fetch(pl.ds(start * block, count * block), weights, sems)
        for copy in copies:
            copy.start()
    if ahead:
        later = fetch(pl.ds(ahead[0] * block, ahead[1] * block), loaded, scratch.pop())
    if held:
        for copy in later:
            copy.start()
    me = lax.axis_index("row")
    place, core = me // 2, me % 2
    for step in range(outer):
        there = (place + outer - step) % outer * 2
        mine = pl.multiple_of((there + core) * rows, rows)
        other = pl.multiple_of((there + 1 - core) * rows, rows)
        for k in range(2):
            grads[k, pl.ds(mine, rows), :] = pieces[step][k]
            grads[k, pl.ds(other, rows), :] = pieces[outer][step, k]
    if first:
        xt_ref[...] = x_ref[...].T
    if write:
        products, sems = scratch
        writes = weight_terms(block, chunk, xt_ref, grads, grad_outs, products, sems)
    dims = (((1,), (1,)), ((), ()))
    flipped = [] if last else [grads[k].T for k in range(2)]
    deep = 256 if depth % 512 == 0 else 128
    for d in range(depth // deep):
        at = slice(d * deep, (d + 1) * deep)
        index, across = d * deep // half, slice(d * deep % half, d * deep % half + deep)
        if copies and d * deep % half == 0:
            copies[2 * index].wait()
            copies[2 * index + 1].wait()
            for copy in later[2 * index : 2 * index + 2]:
                copy.start()
        term = None
        if earlier:
            term = earlier[index][:, across] if last else earlier[0][at, :]
        for k in range(2):
            piece = weights[k][at, :]
            if last:
                product = lax.dot_general(grads[k], piece, dims, preferred_element_type=F32)
            else:
                product = jnp.dot(piece, flipped[k], preferred_element_type=F32)
            term = product if term is None else term + product
        if last:
            sums[index][:, across] = term
        elif len(sums) == 1:
            sums[0][at, :] = term
        else:
            sums[index][:, across] = term.T
    for copy in writes + later:
        copy.wait()


def input_part(quarters, block, chunk, weights, held, pieces, acc, final, x, after, write, ahead):
    depth, tokens = x.shape[1], x.shape[0]
    rows = tokens // quarters
    start, count = chunk
    width = count * block
    first, last = acc is None, final == 0
    args = [*weights, *after, *pieces, *([x] if first else acc)]
    in_specs = [WHOLE if held else REMOTE] * 2 + [REMOTE] * len(after)
    in_specs += [WHOLE] * (len(args) - len(in_specs))
    out_shape = [jax.ShapeDtypeStruct((depth, tokens), BF16)] if first else []
    out_shape += [jax.ShapeDtypeStruct((tokens, depth // 2), F32)] * 2 if final <= 1 else [
        jax.ShapeDtypeStruct((depth, tokens), F32)
    ]
    out_shape.append(jax.ShapeDtypeStruct((2, tokens, width), BF16))
    scratch, aliases, room = [], {}, 0
    if not held:
        scratch += [pltpu.VMEM((2, depth, width), BF16), pltpu.SemaphoreType.DMA((2, 2))]
    out_specs = [WHOLE] * len(out_shape)
    if write:
        xt, state, full = write
        args += [] if first else [xt]
        in_specs += [] if first else [WHOLE]
    if ahead:
        (chunk_ahead, sources), ahead = ahead, ahead[0]
        if held:
            args += [in_hbm(value) for value in sources]
            in_specs += [REMOTE] * 2
    if write:
        aliases = {len(args) + k: len(out_shape) + k for k in range(len(state))}
        args += [in_hbm(value) for value in state]
        in_specs += [REMOTE] * len(state)
        out_shape += [pltpu.HBM((depth, full), BF16)] * 2
        out_specs += [REMOTE] * 2
        scratch += [pltpu.VMEM((2, count, depth, block), BF16), pltpu.SemaphoreType.DMA((2, count))]
    if ahead:
        out_shape += [jax.ShapeDtypeStruct((depth, ahead[1] * block), BF16)] * 2
        out_specs += [WHOLE] * 2
        scratch.append(pltpu.SemaphoreType.DMA((2, 2)))
    if held or ahead:
        room = 4 * depth * max(width, ahead[1] * block if ahead else 0)
    old = 0 if first else len(acc)
    layout = (quarters, rows, block, chunk, held, first, last, len(after), bool(write), old, ahead)
    out = call(
        functools.partial(input_kernel, layout, len(args), len(out_shape)),
        "input_part",
        in_specs,
        out_specs,
        out_shape,
        scratch,
        tokens * depth * (1 if first else width),
        args,
        aliases,
        room,
    )
    out = list(out)
    xt = out.pop(0) if first else None
    fetched = [out.pop() for _ in range(2)][::-1] if ahead else None
    state = [out.pop() for _ in range(2)][::-1] if write else None
    return xt, out[:-1], out[-1], state, fetched


def weight_terms(block, chunk, xt_ref, grads_ref, outs, products, sems):
    start, count = chunk
    xt = xt_ref[...]
    copies = []
    for j in range(count):
        for k, out in enumerate(outs):
            piece = grads_ref[k, :, j * block : (j + 1) * block]
            products[k, j] = jnp.dot(xt, piece, preferred_element_type=F32).astype(BF16)
            copy = pltpu.make_async_copy(
                products.at[k, j], out.at[:, pl.ds((start + j) * block, block)], sems.at[k, j]
            )
            copy.start()
            copies.append(copy)
    return copies


def weight_kernel(block, chunk, skipped, xt_ref, grads_ref, *refs):
    *outs, products, sems = refs[skipped:]
    for copy in weight_terms(block, chunk, xt_ref, grads_ref, outs, products, sems):
        copy.wait()


def weight_part(block, chunk, full, xt, grads, state, after):
    depth, tokens = xt.shape
    count = chunk[1]
    args = [xt, grads, *after, *[in_hbm(value) for value in state]]
    first = len(args) - len(state)
    return call(
        functools.partial(weight_kernel, block, chunk, len(args) - 2),
        "weight_part",
        [WHOLE] * 2 + [REMOTE] * (len(args) - 2),
        [REMOTE] * 2,
        [pltpu.HBM((depth, full), BF16)] * 2,
        [pltpu.VMEM((2, count, depth, block), BF16), pltpu.SemaphoreType.DMA((2, count))],
        tokens * depth * count * block,
        args,
        {first + k: k for k in range(len(state))},
    )


def token_sums(halves, columns, orders):
    position = lax.axis_index("col")
    bits = len(orders[0])
    rows = halves[0].shape[0] // columns
    halves = [half.reshape((2,) * bits + (rows, half.shape[1])) for half in halves]
    lefts = [list(reversed(range(bits))) for _ in halves]
    stages = []
    for stage in range(bits):
        kept, got = [], []
        for half, left, order in zip(halves, lefts, orders):
            bit = order[stage]
            axis = left.index(bit)
            left.remove(bit)
            mine = (position // 2**bit) % 2
            send = lax.dynamic_index_in_dim(half, 1 - mine, axis, keepdims=False)
            moves = [(c, c ^ 2**bit) for c in range(columns)]
            got.append(lax.ppermute(send.astype(BF16), "col", moves))
            kept.append(lax.dynamic_index_in_dim(half, mine, axis, keepdims=False))
        halves = [keep + far.astype(F32) for keep, far in zip(kept, got)]
        stages.append(halves)
    return stages


def local(quarters, columns, inputs, gate_weight, up_weight, hidden_grad):
    outer = quarters // 2
    full = gate_weight.shape[1]
    block, chunks = chunk_list(full)
    swap = [(r, r ^ 1) for r in range(quarters)]

    def sibling(value):
        return lax.ppermute(value, "row", swap)

    def across(value, step):
        moves = [(r, (r // 2 + step) % outer * 2 + r % 2) for r in range(quarters)]
        return lax.ppermute(value, "row", moves)

    number = len(chunks)
    both = [gate_weight, up_weight]
    owns, gots, sums, crossed, pieces, groups, grads = [], [], [], [], [], [], []
    held, flipped = {}, []

    def forward(i, x, early):
        following = chunks[i + 1][0] if i + 1 < number else None
        after = sums[i - 1][:1] if i else []
        own, far, send, *loaded = forward_part(
            quarters, block, chunks[i], following, x, gate_weight, up_weight, early, after
        )
        owns.append(own)
        if i == 0:
            x, loaded = loaded[0], loaded[1:]
        else:
            after = crossed[i - 1][:1] + pieces[i - 1][:1]
            if i == number - 1 and i > 1:
                relay(0, sums[-1][:1])
                take_input(0, x, None, [])
                after += pieces[i - 2][1:2] + grads
            send = in_order(send, after)
        got = sibling(send)
        near = [(far[step - 1] + got[step].astype(F32)).astype(BF16) for step in range(1, outer)]
        gots.append(got)
        sums.append(near)
        crossed.append([across(value, step + 1) for step, value in enumerate(near)])
        return x, loaded

    def middle(i, hidden, after):
        start, count = chunks[i]
        at = slice(start * block, (start + count) * block)
        hidden, mine = middle_part(
            outer, at, owns[i], gots[i], crossed[i], hidden_grad, hidden, after
        )
        pieces.append([mine] + [across(mine, step) for step in range(1, outer)])
        return hidden

    def relay(i, after):
        groups.append(pieces[i] + [sibling(packed(pieces[i], after))])

    def take_input(i, x, acc, after):
        weights = held[i] if i in held else [in_hbm(value) for value in both]
        write = (flipped[0] if i else None, state, full) if i < number - 2 else None
        ahead = (chunks[2], both) if i == 0 and number > 2 else None
        xt, total, whole, written, fetched = input_part(
            quarters, block, chunks[i], weights, i in held, groups[i], acc, number - 1 - i, x,
            after, write, ahead,
        )
        if i == 0:
            flipped.append(xt)
            totals.append(total)
        if written:
            state[:] = written
        if fetched:
            held[2] = fetched
        grads.append(whole)
        return total

    totals, state = [], []
    x, early, hidden, acc = inputs, [], None, None
    for i in range(number):
        x, early = forward(i, x, early)
        hidden = middle(i, hidden, [])
    for i in range(number):
        if i == 0 and grads:
            acc = totals[0]
            continue
        relay(i, grads[1:2] if i > 1 else pieces[-1][:1])
        acc = take_input(i, x, acc, pieces[-1][:1] if 0 < i < number - 1 else [])
    bits = columns.bit_length() - 1
    order = list(range(bits))
    orders = [order[:1] + order[2:] + order[1:2], order[1::-1] + order[2:]]
    stages = [acc] + token_sums(acc, columns, orders)
    input_grad = jnp.concatenate([half.astype(BF16) for half in stages[-1]], axis=1)
    for i in range(max(number - 2, 0), number):
        after = stages[min(i - max(number - 2, 0), bits)]
        state = weight_part(block, chunks[i], full, flipped[0], grads[i], state, after)
    return hidden, input_grad, state[0], state[1]


def solution(mesh):
    return jax.shard_map(
        functools.partial(local, mesh.shape["row"], mesh.shape["col"]),
        mesh=mesh,
        in_specs=(P(None, "row"), P("row", "col"), P("row", "col"), P("row", "col")),
        out_specs=(P("row", "col"), P("col", "row"), P("row", "col"), P("row", "col")),
        check_vma=False,
    )
```

```python
import functools
import math

import jax
import jax.numpy as jnp
from jax import lax
from jax.experimental import pallas as pl
from jax.experimental.pallas import tpu as pltpu
from jax.sharding import PartitionSpec as P

BF16 = jnp.bfloat16
F32 = jnp.float32
VMEM_BYTES = 6 * 1024 * 1024
SHARES = (2, 4, 5, 3)
SLOTS = 3
COST = 40
WHOLE = pl.BlockSpec(memory_space=pltpu.VMEM)
REMOTE = pl.BlockSpec(memory_space=pl.ANY)


def chunk_list(width):
    block = 256 if width % 256 == 0 else 128
    units = width // block
    total = sum(SHARES)
    edges = [0]
    run = 0
    for share in SHARES:
        run += share
        edges.append(max(min(units, round(units * run / total)), edges[-1]))
    return block, [(a, b - a) for a, b in zip(edges, edges[1:]) if b > a]


def call(kernel, name, in_specs, out_specs, out_shape, scratch, size, args, aliases=None, room=0):
    held = [item for item in scratch if len(getattr(item, 'shape', ())) > 2]
    room += VMEM_BYTES + sum(math.prod(item.shape) * item.dtype.itemsize for item in held)
    return pl.pallas_call(
        kernel,
        in_specs=in_specs,
        out_specs=out_specs,
        out_shape=out_shape,
        scratch_shapes=scratch,
        input_output_aliases=aliases or {},
        compiler_params=pltpu.CompilerParams(vmem_limit_bytes=room),
        cost_estimate=pl.CostEstimate(
            flops=COST * size, bytes_accessed=size, transcendentals=0
        ),
        name=name,
    )(*args)


def in_hbm(value):
    return pltpu.with_memory_space_constraint(value, pltpu.HBM)


def in_order(value, after):
    return call(
        lambda *refs: None,
        "in_order",
        [REMOTE] * (1 + len(after)),
        REMOTE,
        jax.ShapeDtypeStruct(value.shape, value.dtype),
        [],
        1,
        [value, *after],
        {0: 0},
    )


def pack_kernel(count, *refs):
    for step, ref in enumerate(refs[:count]):
        refs[-1][step] = ref[...]


def packed(values, after):
    return call(
        functools.partial(pack_kernel, len(values)),
        "packed",
        [WHOLE] * len(values) + [REMOTE] * len(after),
        WHOLE,
        jax.ShapeDtypeStruct((len(values), *values[0].shape), values[0].dtype),
        [],
        1,
        [*values, *after],
    )


def forward_kernel(layout, ins, outs, *refs):
    quarters, rows, block, start, count, following, first = layout
    given, made = refs[:ins], refs[ins : ins + outs]
    weights, total, sems, x_sem = refs[ins + outs :]
    sources = given[1:3]
    own_ref, far_ref, send_ref, *made = made
    x_ref, early = given[0], given[3:5]
    if first:
        x_copy = pltpu.make_async_copy(x_ref, made[0], x_sem)
        x_copy.start()
        x_ref, made = made[0], made[1:]
    slots = weights.shape[1]
    queue = [
        [
            pltpu.make_async_copy(
                source.at[:, pl.ds((start + j) * block, block)],
                weights.at[k, j % slots],
                sems.at[k, j % slots],
            )
            for k, source in enumerate(sources)
        ]
        for j in range(0 if first else 1, count)
    ]
    if made:
        queue.append(
            [
                pltpu.make_async_copy(
                    source.at[:, pl.ds(following * block, block)], target, sems.at[k, slots]
                )
                for k, (source, target) in enumerate(zip(sources, made))
            ]
        )
    for pair in queue[: slots - 1]:
        for copy in pair:
            copy.start()
    if first:
        x_copy.wait()
    outer = quarters // 2
    me = lax.axis_index("row")
    place, core = me // 2, me % 2
    x = x_ref[...]
    taken = 0
    for j in range(count):
        at = slice(j * block, (j + 1) * block)
        if first or j:
            for copy in queue[taken]:
                copy.wait()
            taken += 1
            more = taken + slots - 2
            for copy in queue[more] if more < len(queue) else []:
                copy.start()
            blocks = [weights[k, j % slots] for k in range(2)]
        else:
            blocks = [ref[...] for ref in early]
        for k in range(2):
            total[k] = jnp.dot(x, blocks[k], preferred_element_type=F32)
        for step in range(outer):
            there = (place + step) % outer * 2
            mine = pl.multiple_of((there + core) * rows, rows)
            other = pl.multiple_of((there + 1 - core) * rows, rows)
            for k in range(2):
                kept = total[k, pl.ds(mine, rows), :]
                if step == 0:
                    own_ref[k, :, at] = kept
                else:
                    far_ref[step - 1, k, :, at] = kept
                send_ref[step, k, :, at] = total[k, pl.ds(other, rows), :].astype(BF16)
    for pair in queue[taken:]:
        for copy in pair:
            copy.wait()


def forward_part(quarters, block, chunk, following, x, gate_weight, up_weight, early, after):
    tokens, depth = x.shape
    rows = tokens // quarters
    outer = quarters // 2
    start, count = chunk
    width = count * block
    first = not early
    out_shape = [
        jax.ShapeDtypeStruct((2, rows, width), F32),
        jax.ShapeDtypeStruct((outer - 1, 2, rows, width), F32),
        jax.ShapeDtypeStruct((outer, 2, rows, width), BF16),
    ]
    if first:
        x = in_hbm(x)
        out_shape.append(jax.ShapeDtypeStruct(x.shape, BF16))
    if following is not None:
        out_shape += [jax.ShapeDtypeStruct((depth, block), BF16)] * 2
    args = (x, in_hbm(gate_weight), in_hbm(up_weight), *early, *after)
    layout = (quarters, rows, block, start, count, following, first)
    return call(
        functools.partial(forward_kernel, layout, len(args), len(out_shape)),
        "forward_part",
        [REMOTE if first else WHOLE, REMOTE, REMOTE]
        + [WHOLE] * len(early)
        + [REMOTE] * len(after),
        [WHOLE] * len(out_shape),
        out_shape,
        [
            pltpu.VMEM((2, SLOTS, depth, block), BF16),
            pltpu.VMEM((2, tokens, block), F32),
            pltpu.SemaphoreType.DMA((2, SLOTS + 1)),
            pltpu.SemaphoreType.DMA,
        ],
        tokens * depth * width,
        args,
    )


def middle_kernel(outer, at, first, skipped, own_ref, got_ref, upstream_ref, *refs):
    far_refs, rest = refs[: outer - 1], refs[outer - 1 + skipped :]
    if not first:
        rest[1][...] = rest[0][...]
        rest = rest[1:]
    hidden_ref, grads_ref = rest
    gate_pre = own_ref[0] + got_ref[0, 0].astype(F32)
    up_pre = own_ref[1] + got_ref[0, 1].astype(F32)
    for far in far_refs:
        gate_pre += far[0].astype(F32)
        up_pre += far[1].astype(F32)
    sigma_gate = jax.nn.sigmoid(gate_pre)
    upstream = upstream_ref[:, at].astype(F32)
    gated = gate_pre * sigma_gate
    hidden_ref[:, at] = (gated * up_pre).astype(BF16)
    slope = sigma_gate * (1.0 + gate_pre * (1.0 - sigma_gate))
    grads_ref[0] = (upstream * up_pre * slope).astype(BF16)
    grads_ref[1] = (upstream * gated).astype(BF16)


def middle_part(outer, at, own, got, far, hidden_grad, hidden, after):
    rows, width = own.shape[1:]
    first = hidden is None
    args = [own, got, hidden_grad, *far, *after] + ([] if first else [hidden])
    return call(
        functools.partial(middle_kernel, outer, at, first, len(after)),
        "middle_part",
        [WHOLE] * (2 + outer) + [REMOTE] * len(after) + [WHOLE] * (not first),
        [WHOLE] * 2,
        [
            jax.ShapeDtypeStruct(hidden_grad.shape, BF16),
            jax.ShapeDtypeStruct((2, rows, width), BF16),
        ],
        [],
        rows * width,
        args,
    )


def input_kernel(layout, ins, outs, *refs):
    quarters, rows, block, chunk, held, first, last, skipped, write, old, ahead = layout
    given, made, scratch = refs[:ins], list(refs[ins : ins + outs]), list(refs[ins + outs :])
    (gate_ref, up_ref), given = given[:2], given[2 + skipped :]
    outer = quarters // 2
    pieces, given = given[: outer + 1], list(given[outer + 1 :])
    sources = (gate_ref, up_ref)
    depth = gate_ref.shape[0]
    half = depth // 2
    earlier = []
    if first:
        x_ref, xt_ref = given.pop(0), made.pop(0)
    else:
        earlier = [given.pop(0) for _ in range(old)]
    if write and not first:
        xt_ref = given.pop(0)
    if ahead and held:
        sources = (given.pop(0), given.pop(0))
    loaded = [made.pop() for _ in range(2)][::-1] if ahead else []
    grad_outs = [made.pop() for _ in range(2)][::-1] if write else []
    grads = made.pop()
    sums = made

    def fetch(columns, targets, sems):
        return [
            pltpu.make_async_copy(
                source.at[pl.ds(h * half, half), columns],
                target.at[pl.ds(h * half, half)],
                sems.at[k, h],
            )
            for h in range(2)
            for k, (source, target) in enumerate(zip(sources, targets))
        ]

    weights, copies, later, writes = (gate_ref, up_ref), [], [], []
    start, count = chunk
    if not held:
        store, sems = scratch.pop(0), scratch.pop(0)
        weights = (store.at[0], store.at[1])
        copies = fetch(pl.ds(start * block, count * block), weights, sems)
        for copy in copies:
            copy.start()
    if ahead:
        later = fetch(pl.ds(ahead[0] * block, ahead[1] * block), loaded, scratch.pop())
    if held:
        for copy in later:
            copy.start()
    me = lax.axis_index("row")
    place, core = me // 2, me % 2
    for step in range(outer):
        there = (place + outer - step) % outer * 2
        mine = pl.multiple_of((there + core) * rows, rows)
        other = pl.multiple_of((there + 1 - core) * rows, rows)
        for k in range(2):
            grads[k, pl.ds(mine, rows), :] = pieces[step][k]
            grads[k, pl.ds(other, rows), :] = pieces[outer][step, k]
    if first:
        xt_ref[...] = x_ref[...].T
    if write:
        products, sems = scratch
        writes = weight_terms(block, chunk, xt_ref, grads, grad_outs, products, sems)
    dims = (((1,), (1,)), ((), ()))
    flipped = [] if last else [grads[k].T for k in range(2)]
    deep = 256 if depth % 512 == 0 else 128
    for d in range(depth // deep):
        at = slice(d * deep, (d + 1) * deep)
        index, across = d * deep // half, slice(d * deep % half, d * deep % half + deep)
        if copies and d * deep % half == 0:
            copies[2 * index].wait()
            copies[2 * index + 1].wait()
            for copy in later[2 * index : 2 * index + 2]:
                copy.start()
        term = None
        if earlier:
            term = earlier[index][:, across] if last else earlier[0][at, :]
        for k in range(2):
            piece = weights[k][at, :]
            if last:
                product = lax.dot_general(grads[k], piece, dims, preferred_element_type=F32)
            else:
                product = jnp.dot(piece, flipped[k], preferred_element_type=F32)
            term = product if term is None else term + product
        if last:
            sums[index][:, across] = term
        elif len(sums) == 1:
            sums[0][at, :] = term
        else:
            sums[index][:, across] = term.T
    for copy in writes + later:
        copy.wait()


def input_part(quarters, block, chunk, weights, held, pieces, acc, final, x, after, write, ahead):
    depth, tokens = x.shape[1], x.shape[0]
    rows = tokens // quarters
    start, count = chunk
    width = count * block
    first, last = acc is None, final == 0
    args = [*weights, *after, *pieces, *([x] if first else acc)]
    in_specs = [WHOLE if held else REMOTE] * 2 + [REMOTE] * len(after)
    in_specs += [WHOLE] * (len(args) - len(in_specs))
    out_shape = [jax.ShapeDtypeStruct((depth, tokens), BF16)] if first else []
    out_shape += [jax.ShapeDtypeStruct((tokens, depth // 2), F32)] * 2 if final <= 1 else [
        jax.ShapeDtypeStruct((depth, tokens), F32)
    ]
    out_shape.append(jax.ShapeDtypeStruct((2, tokens, width), BF16))
    scratch, aliases, room = [], {}, 0
    if not held:
        scratch += [pltpu.VMEM((2, depth, width), BF16), pltpu.SemaphoreType.DMA((2, 2))]
    out_specs = [WHOLE] * len(out_shape)
    if write:
        xt, state, full = write
        args += [] if first else [xt]
        in_specs += [] if first else [WHOLE]
    if ahead:
        (chunk_ahead, sources), ahead = ahead, ahead[0]
        if held:
            args += [in_hbm(value) for value in sources]
            in_specs += [REMOTE] * 2
    if write:
        aliases = {len(args) + k: len(out_shape) + k for k in range(len(state))}
        args += [in_hbm(value) for value in state]
        in_specs += [REMOTE] * len(state)
        out_shape += [pltpu.HBM((depth, full), BF16)] * 2
        out_specs += [REMOTE] * 2
        scratch += [pltpu.VMEM((2, count, depth, block), BF16), pltpu.SemaphoreType.DMA((2, count))]
    if ahead:
        out_shape += [jax.ShapeDtypeStruct((depth, ahead[1] * block), BF16)] * 2
        out_specs += [WHOLE] * 2
        scratch.append(pltpu.SemaphoreType.DMA((2, 2)))
    if held or ahead:
        room = 4 * depth * max(width, ahead[1] * block if ahead else 0)
    old = 0 if first else len(acc)
    layout = (quarters, rows, block, chunk, held, first, last, len(after), bool(write), old, ahead)
    out = call(
        functools.partial(input_kernel, layout, len(args), len(out_shape)),
        "input_part",
        in_specs,
        out_specs,
        out_shape,
        scratch,
        tokens * depth * (1 if first else width),
        args,
        aliases,
        room,
    )
    out = list(out)
    xt = out.pop(0) if first else None
    fetched = [out.pop() for _ in range(2)][::-1] if ahead else None
    state = [out.pop() for _ in range(2)][::-1] if write else None
    return xt, out[:-1], out[-1], state, fetched


def weight_terms(block, chunk, xt_ref, grads_ref, outs, products, sems):
    start, count = chunk
    xt = xt_ref[...]
    copies = []
    for j in range(count):
        for k, out in enumerate(outs):
            piece = grads_ref[k, :, j * block : (j + 1) * block]
            products[k, j] = jnp.dot(xt, piece, preferred_element_type=F32).astype(BF16)
            copy = pltpu.make_async_copy(
                products.at[k, j], out.at[:, pl.ds((start + j) * block, block)], sems.at[k, j]
            )
            copy.start()
            copies.append(copy)
    return copies


def weight_kernel(block, chunk, skipped, xt_ref, grads_ref, *refs):
    *outs, products, sems = refs[skipped:]
    for copy in weight_terms(block, chunk, xt_ref, grads_ref, outs, products, sems):
        copy.wait()


def weight_part(block, chunk, full, xt, grads, state, after):
    depth, tokens = xt.shape
    count = chunk[1]
    args = [xt, grads, *after, *[in_hbm(value) for value in state]]
    first = len(args) - len(state)
    return call(
        functools.partial(weight_kernel, block, chunk, len(args) - 2),
        "weight_part",
        [WHOLE] * 2 + [REMOTE] * (len(args) - 2),
        [REMOTE] * 2,
        [pltpu.HBM((depth, full), BF16)] * 2,
        [pltpu.VMEM((2, count, depth, block), BF16), pltpu.SemaphoreType.DMA((2, count))],
        tokens * depth * count * block,
        args,
        {first + k: k for k in range(len(state))},
    )


def token_sums(halves, columns, orders):
    position = lax.axis_index("col")
    bits = len(orders[0])
    rows = halves[0].shape[0] // columns
    halves = [half.reshape((2,) * bits + (rows, half.shape[1])) for half in halves]
    lefts = [list(reversed(range(bits))) for _ in halves]
    stages = []
    for stage in range(bits):
        kept, got = [], []
        for half, left, order in zip(halves, lefts, orders):
            bit = order[stage]
            axis = left.index(bit)
            left.remove(bit)
            mine = (position // 2**bit) % 2
            send = lax.dynamic_index_in_dim(half, 1 - mine, axis, keepdims=False)
            moves = [(c, c ^ 2**bit) for c in range(columns)]
            got.append(lax.ppermute(send.astype(BF16), "col", moves))
            kept.append(lax.dynamic_index_in_dim(half, mine, axis, keepdims=False))
        halves = [keep + far.astype(F32) for keep, far in zip(kept, got)]
        stages.append(halves)
    return stages


def local(quarters, columns, inputs, gate_weight, up_weight, hidden_grad):
    outer = quarters // 2
    full = gate_weight.shape[1]
    block, chunks = chunk_list(full)
    swap = [(r, r ^ 1) for r in range(quarters)]

    def sibling(value):
        return lax.ppermute(value, "row", swap)

    def across(value, step):
        moves = [(r, (r // 2 + step) % outer * 2 + r % 2) for r in range(quarters)]
        return lax.ppermute(value, "row", moves)

    number = len(chunks)
    both = [gate_weight, up_weight]
    owns, gots, sums, crossed, pieces, groups, grads = [], [], [], [], [], [], []
    held, flipped = {}, []

    def forward(i, x, early):
        following = chunks[i + 1][0] if i + 1 < number else None
        after = sums[i - 1][:1] if i else []
        own, far, send, *loaded = forward_part(
            quarters, block, chunks[i], following, x, gate_weight, up_weight, early, after
        )
        owns.append(own)
        if i == 0:
            x, loaded = loaded[0], loaded[1:]
        elif i < 3:
            send = in_order(send, crossed[i - 1][:1] + pieces[i - 1][:1])
        else:
            if i == number - 1:
                relay(0, sums[-1][:1])
                take_input(0, x, None, [])
            send = in_order(send, crossed[i - 1][:1] + pieces[i - 1][:1] + pieces[i - 2][1:2] + grads)
        got = sibling(send)
        near = [(far[step - 1] + got[step].astype(F32)).astype(BF16) for step in range(1, outer)]
        gots.append(got)
        sums.append(near)
        crossed.append([across(value, step + 1) for step, value in enumerate(near)])
        return x, loaded

    def middle(i, hidden, after):
        start, count = chunks[i]
        at = slice(start * block, (start + count) * block)
        hidden, mine = middle_part(
            outer, at, owns[i], gots[i], crossed[i], hidden_grad, hidden, after
        )
        pieces.append([mine] + [across(mine, step) for step in range(1, outer)])
        return hidden

    def relay(i, after):
        groups.append(pieces[i] + [sibling(packed(pieces[i], after))])

    def take_input(i, x, acc, after):
        weights = held[i] if i in held else [in_hbm(value) for value in both]
        write = (flipped[0] if i else None, state, full) if i < number - 2 else None
        ahead = (chunks[2], both) if i == 0 and number > 2 else None
        xt, total, whole, written, fetched = input_part(
            quarters, block, chunks[i], weights, i in held, groups[i], acc, number - 1 - i, x,
            after, write, ahead,
        )
        if i == 0:
            flipped.append(xt)
            totals.append(total)
        if written:
            state[:] = written
        if fetched:
            held[2] = fetched
        grads.append(whole)
        return total

    totals, state = [], []
    x, early, hidden = inputs, [], None
    for i in range(number):
        x, early = forward(i, x, early)
        if i < 3:
            hidden = middle(i, hidden, pieces[0][1:2] if i == 2 else [])
    acc = None
    for i in range(number):
        if i == 0 and grads:
            acc = totals[0]
            continue
        after = sums[-1][:1] + pieces[i + 1][:1] if i == 1 and number > 3 else []
        relay(i, grads[-1:] + pieces[-1][:1] if i > 1 else sums[-1][:1])
        acc = take_input(i, x, acc, after)
        for j in range(len(pieces), number if i else 0):
            hidden = middle(j, hidden, grads[-1:])
    bits = columns.bit_length() - 1
    order = list(range(bits))
    orders = [order[:1] + order[2:] + order[1:2], order[1::-1] + order[2:]]
    stages = [acc] + token_sums(acc, columns, orders)
    input_grad = jnp.concatenate([half.astype(BF16) for half in stages[-1]], axis=1)
    for i in range(max(number - 2, 0), number):
        after = stages[min(i - max(number - 2, 0), bits)]
        state = weight_part(block, chunks[i], full, flipped[0], grads[i], state, after)
    return hidden, input_grad, state[0], state[1]


def solution(mesh):
    return jax.shard_map(
        functools.partial(local, mesh.shape["row"], mesh.shape["col"]),
        mesh=mesh,
        in_specs=(P(None, "row"), P("row", "col"), P("row", "col"), P("row", "col")),
        out_specs=(P("row", "col"), P("col", "row"), P("row", "col"), P("row", "col")),
        check_vma=False,
    )
```

```python
import functools
import math

import jax
import jax.numpy as jnp
from jax import lax
from jax.experimental import pallas as pl
from jax.experimental.pallas import tpu as pltpu
from jax.sharding import PartitionSpec as P

BF16 = jnp.bfloat16
F32 = jnp.float32
VMEM_BYTES = 6 * 1024 * 1024
SHARES = (2, 4, 5, 3)
SLOTS = 3
COST = 40
WHOLE = pl.BlockSpec(memory_space=pltpu.VMEM)
REMOTE = pl.BlockSpec(memory_space=pl.ANY)


def chunk_list(width):
    block = 256 if width % 256 == 0 else 128
    units = width // block
    total = sum(SHARES)
    edges = [0]
    run = 0
    for share in SHARES:
        run += share
        edges.append(max(min(units, round(units * run / total)), edges[-1]))
    return block, [(a, b - a) for a, b in zip(edges, edges[1:]) if b > a]


def call(kernel, name, in_specs, out_specs, out_shape, scratch, size, args, aliases=None, room=0):
    held = [item for item in scratch if len(getattr(item, 'shape', ())) > 2]
    room += VMEM_BYTES + sum(math.prod(item.shape) * item.dtype.itemsize for item in held)
    return pl.pallas_call(
        kernel,
        in_specs=in_specs,
        out_specs=out_specs,
        out_shape=out_shape,
        scratch_shapes=scratch,
        input_output_aliases=aliases or {},
        compiler_params=pltpu.CompilerParams(vmem_limit_bytes=room),
        cost_estimate=pl.CostEstimate(
            flops=COST * size, bytes_accessed=size, transcendentals=0
        ),
        name=name,
    )(*args)


def in_hbm(value):
    return pltpu.with_memory_space_constraint(value, pltpu.HBM)


def in_order(value, after):
    return call(
        lambda *refs: None,
        "in_order",
        [REMOTE] * (1 + len(after)),
        REMOTE,
        jax.ShapeDtypeStruct(value.shape, value.dtype),
        [],
        1,
        [value, *after],
        {0: 0},
    )


def pack_kernel(count, *refs):
    for step, ref in enumerate(refs[:count]):
        refs[-1][step] = ref[...]


def packed(values, after):
    return call(
        functools.partial(pack_kernel, len(values)),
        "packed",
        [WHOLE] * len(values) + [REMOTE] * len(after),
        WHOLE,
        jax.ShapeDtypeStruct((len(values), *values[0].shape), values[0].dtype),
        [],
        1,
        [*values, *after],
    )


def forward_kernel(layout, ins, outs, *refs):
    quarters, rows, block, start, count, following, first = layout
    given, made = refs[:ins], refs[ins : ins + outs]
    weights, total, sems, x_sem = refs[ins + outs :]
    sources = given[1:3]
    own_ref, far_ref, send_ref, *made = made
    x_ref, early = given[0], given[3:5]
    if first:
        x_copy = pltpu.make_async_copy(x_ref, made[0], x_sem)
        x_copy.start()
        x_ref, made = made[0], made[1:]
    slots = weights.shape[1]
    queue = [
        [
            pltpu.make_async_copy(
                source.at[:, pl.ds((start + j) * block, block)],
                weights.at[k, j % slots],
                sems.at[k, j % slots],
            )
            for k, source in enumerate(sources)
        ]
        for j in range(0 if first else 1, count)
    ]
    if made:
        queue.append(
            [
                pltpu.make_async_copy(
                    source.at[:, pl.ds(following * block, block)], target, sems.at[k, slots]
                )
                for k, (source, target) in enumerate(zip(sources, made))
            ]
        )
    for pair in queue[: slots - 1]:
        for copy in pair:
            copy.start()
    if first:
        x_copy.wait()
    outer = quarters // 2
    me = lax.axis_index("row")
    place, core = me // 2, me % 2
    x = x_ref[...]
    taken = 0
    for j in range(count):
        at = slice(j * block, (j + 1) * block)
        if first or j:
            for copy in queue[taken]:
                copy.wait()
            taken += 1
            more = taken + slots - 2
            for copy in queue[more] if more < len(queue) else []:
                copy.start()
            blocks = [weights[k, j % slots] for k in range(2)]
        else:
            blocks = [ref[...] for ref in early]
        for k in range(2):
            total[k] = jnp.dot(x, blocks[k], preferred_element_type=F32)
        for step in range(outer):
            there = (place + step) % outer * 2
            mine = pl.multiple_of((there + core) * rows, rows)
            other = pl.multiple_of((there + 1 - core) * rows, rows)
            for k in range(2):
                kept = total[k, pl.ds(mine, rows), :]
                if step == 0:
                    own_ref[k, :, at] = kept
                else:
                    far_ref[step - 1, k, :, at] = kept
                send_ref[step, k, :, at] = total[k, pl.ds(other, rows), :].astype(BF16)
    for pair in queue[taken:]:
        for copy in pair:
            copy.wait()


def forward_part(quarters, block, chunk, following, x, gate_weight, up_weight, early, after):
    tokens, depth = x.shape
    rows = tokens // quarters
    outer = quarters // 2
    start, count = chunk
    width = count * block
    first = not early
    out_shape = [
        jax.ShapeDtypeStruct((2, rows, width), F32),
        jax.ShapeDtypeStruct((outer - 1, 2, rows, width), F32),
        jax.ShapeDtypeStruct((outer, 2, rows, width), BF16),
    ]
    if first:
        x = in_hbm(x)
        out_shape.append(jax.ShapeDtypeStruct(x.shape, BF16))
    if following is not None:
        out_shape += [jax.ShapeDtypeStruct((depth, block), BF16)] * 2
    args = (x, in_hbm(gate_weight), in_hbm(up_weight), *early, *after)
    layout = (quarters, rows, block, start, count, following, first)
    return call(
        functools.partial(forward_kernel, layout, len(args), len(out_shape)),
        "forward_part",
        [REMOTE if first else WHOLE, REMOTE, REMOTE]
        + [WHOLE] * len(early)
        + [REMOTE] * len(after),
        [WHOLE] * len(out_shape),
        out_shape,
        [
            pltpu.VMEM((2, SLOTS, depth, block), BF16),
            pltpu.VMEM((2, tokens, block), F32),
            pltpu.SemaphoreType.DMA((2, SLOTS + 1)),
            pltpu.SemaphoreType.DMA,
        ],
        tokens * depth * width,
        args,
    )


def middle_kernel(outer, at, first, skipped, own_ref, got_ref, upstream_ref, *refs):
    far_refs, rest = refs[: outer - 1], refs[outer - 1 + skipped :]
    if not first:
        rest[1][...] = rest[0][...]
        rest = rest[1:]
    hidden_ref, grads_ref = rest
    gate_pre = own_ref[0] + got_ref[0, 0].astype(F32)
    up_pre = own_ref[1] + got_ref[0, 1].astype(F32)
    for far in far_refs:
        gate_pre += far[0].astype(F32)
        up_pre += far[1].astype(F32)
    sigma_gate = jax.nn.sigmoid(gate_pre)
    upstream = upstream_ref[:, at].astype(F32)
    gated = gate_pre * sigma_gate
    hidden_ref[:, at] = (gated * up_pre).astype(BF16)
    slope = sigma_gate * (1.0 + gate_pre * (1.0 - sigma_gate))
    grads_ref[0] = (upstream * up_pre * slope).astype(BF16)
    grads_ref[1] = (upstream * gated).astype(BF16)


def middle_part(outer, at, own, got, far, hidden_grad, hidden, after):
    rows, width = own.shape[1:]
    first = hidden is None
    args = [own, got, hidden_grad, *far, *after] + ([] if first else [hidden])
    return call(
        functools.partial(middle_kernel, outer, at, first, len(after)),
        "middle_part",
        [WHOLE] * (2 + outer) + [REMOTE] * len(after) + [WHOLE] * (not first),
        [WHOLE] * 2,
        [
            jax.ShapeDtypeStruct(hidden_grad.shape, BF16),
            jax.ShapeDtypeStruct((2, rows, width), BF16),
        ],
        [],
        rows * width,
        args,
    )


def input_kernel(layout, ins, outs, *refs):
    quarters, rows, block, chunk, held, first, last, skipped, write, old, ahead = layout
    given, made, scratch = refs[:ins], list(refs[ins : ins + outs]), list(refs[ins + outs :])
    (gate_ref, up_ref), given = given[:2], given[2 + skipped :]
    outer = quarters // 2
    pieces, given = given[: outer + 1], list(given[outer + 1 :])
    sources = (gate_ref, up_ref)
    depth = gate_ref.shape[0]
    half = depth // 2
    earlier = []
    if first:
        x_ref, xt_ref = given.pop(0), made.pop(0)
    else:
        earlier = [given.pop(0) for _ in range(old)]
    if write and not first:
        xt_ref = given.pop(0)
    if ahead and held:
        sources = (given.pop(0), given.pop(0))
    loaded = [made.pop() for _ in range(2)][::-1] if ahead else []
    grad_outs = [made.pop() for _ in range(2)][::-1] if write else []
    grads = made.pop()
    sums = made

    def fetch(columns, targets, sems):
        return [
            pltpu.make_async_copy(
                source.at[pl.ds(h * half, half), columns],
                target.at[pl.ds(h * half, half)],
                sems.at[k, h],
            )
            for h in range(2)
            for k, (source, target) in enumerate(zip(sources, targets))
        ]

    weights, copies, later, writes = (gate_ref, up_ref), [], [], []
    start, count = chunk
    if not held:
        store, sems = scratch.pop(0), scratch.pop(0)
        weights = (store.at[0], store.at[1])
        copies = fetch(pl.ds(start * block, count * block), weights, sems)
        for copy in copies:
            copy.start()
    if ahead:
        later = fetch(pl.ds(ahead[0] * block, ahead[1] * block), loaded, scratch.pop())
    if held:
        for copy in later:
            copy.start()
    me = lax.axis_index("row")
    place, core = me // 2, me % 2
    for step in range(outer):
        there = (place + outer - step) % outer * 2
        mine = pl.multiple_of((there + core) * rows, rows)
        other = pl.multiple_of((there + 1 - core) * rows, rows)
        for k in range(2):
            grads[k, pl.ds(mine, rows), :] = pieces[step][k]
            grads[k, pl.ds(other, rows), :] = pieces[outer][step, k]
    if first:
        xt_ref[...] = x_ref[...].T
    if write:
        products, sems = scratch
        writes = weight_terms(block, chunk, xt_ref, grads, grad_outs, products, sems)
    dims = (((1,), (1,)), ((), ()))
    flipped = [] if last else [grads[k].T for k in range(2)]
    deep = 256 if depth % 512 == 0 else 128
    for d in range(depth // deep):
        at = slice(d * deep, (d + 1) * deep)
        index, across = d * deep // half, slice(d * deep % half, d * deep % half + deep)
        if copies and d * deep % half == 0:
            copies[2 * index].wait()
            copies[2 * index + 1].wait()
            for copy in later[2 * index : 2 * index + 2]:
                copy.start()
        term = None
        if earlier:
            term = earlier[index][:, across] if last else earlier[0][at, :]
        for k in range(2):
            piece = weights[k][at, :]
            if last:
                product = lax.dot_general(grads[k], piece, dims, preferred_element_type=F32)
            else:
                product = jnp.dot(piece, flipped[k], preferred_element_type=F32)
            term = product if term is None else term + product
        if last:
            sums[index][:, across] = term
        elif len(sums) == 1:
            sums[0][at, :] = term
        else:
            sums[index][:, across] = term.T
    for copy in writes + later:
        copy.wait()


def input_part(quarters, block, chunk, weights, held, pieces, acc, final, x, after, write, ahead):
    depth, tokens = x.shape[1], x.shape[0]
    rows = tokens // quarters
    start, count = chunk
    width = count * block
    first, last = acc is None, final == 0
    args = [*weights, *after, *pieces, *([x] if first else acc)]
    in_specs = [WHOLE if held else REMOTE] * 2 + [REMOTE] * len(after)
    in_specs += [WHOLE] * (len(args) - len(in_specs))
    out_shape = [jax.ShapeDtypeStruct((depth, tokens), BF16)] if first else []
    out_shape += [jax.ShapeDtypeStruct((tokens, depth // 2), F32)] * 2 if final <= 1 else [
        jax.ShapeDtypeStruct((depth, tokens), F32)
    ]
    out_shape.append(jax.ShapeDtypeStruct((2, tokens, width), BF16))
    scratch, aliases, room = [], {}, 0
    if not held:
        scratch += [pltpu.VMEM((2, depth, width), BF16), pltpu.SemaphoreType.DMA((2, 2))]
    out_specs = [WHOLE] * len(out_shape)
    if write:
        xt, state, full = write
        args += [] if first else [xt]
        in_specs += [] if first else [WHOLE]
    if ahead:
        (chunk_ahead, sources), ahead = ahead, ahead[0]
        if held:
            args += [in_hbm(value) for value in sources]
            in_specs += [REMOTE] * 2
    if write:
        aliases = {len(args) + k: len(out_shape) + k for k in range(len(state))}
        args += [in_hbm(value) for value in state]
        in_specs += [REMOTE] * len(state)
        out_shape += [pltpu.HBM((depth, full), BF16)] * 2
        out_specs += [REMOTE] * 2
        scratch += [pltpu.VMEM((2, count, depth, block), BF16), pltpu.SemaphoreType.DMA((2, count))]
    if ahead:
        out_shape += [jax.ShapeDtypeStruct((depth, ahead[1] * block), BF16)] * 2
        out_specs += [WHOLE] * 2
        scratch.append(pltpu.SemaphoreType.DMA((2, 2)))
    if held or ahead:
        room = 4 * depth * max(width, ahead[1] * block if ahead else 0)
    old = 0 if first else len(acc)
    layout = (quarters, rows, block, chunk, held, first, last, len(after), bool(write), old, ahead)
    out = call(
        functools.partial(input_kernel, layout, len(args), len(out_shape)),
        "input_part",
        in_specs,
        out_specs,
        out_shape,
        scratch,
        tokens * depth * width,
        args,
        aliases,
        room,
    )
    out = list(out)
    xt = out.pop(0) if first else None
    fetched = [out.pop() for _ in range(2)][::-1] if ahead else None
    state = [out.pop() for _ in range(2)][::-1] if write else None
    return xt, out[:-1], out[-1], state, fetched


def weight_terms(block, chunk, xt_ref, grads_ref, outs, products, sems):
    start, count = chunk
    xt = xt_ref[...]
    copies = []
    for j in range(count):
        for k, out in enumerate(outs):
            piece = grads_ref[k, :, j * block : (j + 1) * block]
            products[k, j] = jnp.dot(xt, piece, preferred_element_type=F32).astype(BF16)
            copy = pltpu.make_async_copy(
                products.at[k, j], out.at[:, pl.ds((start + j) * block, block)], sems.at[k, j]
            )
            copy.start()
            copies.append(copy)
    return copies


def weight_kernel(block, chunk, skipped, xt_ref, grads_ref, *refs):
    *outs, products, sems = refs[skipped:]
    for copy in weight_terms(block, chunk, xt_ref, grads_ref, outs, products, sems):
        copy.wait()


def weight_part(block, chunk, full, xt, grads, state, after):
    depth, tokens = xt.shape
    count = chunk[1]
    args = [xt, grads, *after, *[in_hbm(value) for value in state]]
    first = len(args) - len(state)
    return call(
        functools.partial(weight_kernel, block, chunk, len(args) - 2),
        "weight_part",
        [WHOLE] * 2 + [REMOTE] * (len(args) - 2),
        [REMOTE] * 2,
        [pltpu.HBM((depth, full), BF16)] * 2,
        [pltpu.VMEM((2, count, depth, block), BF16), pltpu.SemaphoreType.DMA((2, count))],
        tokens * depth * count * block,
        args,
        {first + k: k for k in range(len(state))},
    )


def token_sums(halves, columns, orders):
    position = lax.axis_index("col")
    bits = len(orders[0])
    rows = halves[0].shape[0] // columns
    halves = [half.reshape((2,) * bits + (rows, half.shape[1])) for half in halves]
    lefts = [list(reversed(range(bits))) for _ in halves]
    stages = []
    for stage in range(bits):
        kept, got = [], []
        for half, left, order in zip(halves, lefts, orders):
            bit = order[stage]
            axis = left.index(bit)
            left.remove(bit)
            mine = (position // 2**bit) % 2
            send = lax.dynamic_index_in_dim(half, 1 - mine, axis, keepdims=False)
            moves = [(c, c ^ 2**bit) for c in range(columns)]
            got.append(lax.ppermute(send.astype(BF16), "col", moves))
            kept.append(lax.dynamic_index_in_dim(half, mine, axis, keepdims=False))
        halves = [keep + far.astype(F32) for keep, far in zip(kept, got)]
        stages.append(halves)
    return stages


def local(quarters, columns, inputs, gate_weight, up_weight, hidden_grad):
    outer = quarters // 2
    full = gate_weight.shape[1]
    block, chunks = chunk_list(full)
    swap = [(r, r ^ 1) for r in range(quarters)]

    def sibling(value):
        return lax.ppermute(value, "row", swap)

    def across(value, step):
        moves = [(r, (r // 2 + step) % outer * 2 + r % 2) for r in range(quarters)]
        return lax.ppermute(value, "row", moves)

    number = len(chunks)
    both = [gate_weight, up_weight]
    owns, gots, sums, crossed, pieces, groups, grads = [], [], [], [], [], [], []
    held, flipped = {}, []

    def forward(i, x, early):
        following = chunks[i + 1][0] if i + 1 < number else None
        after = sums[i - 1][:1] if i else []
        own, far, send, *loaded = forward_part(
            quarters, block, chunks[i], following, x, gate_weight, up_weight, early, after
        )
        owns.append(own)
        if i == 0:
            x, loaded = loaded[0], loaded[1:]
        else:
            after = crossed[i - 1][:1] + pieces[i - 1][:1]
            send = in_order(send, after + (pieces[0][1:2] if i == 3 else []))
        if i > 1 and len(pieces[i - 2]) < outer:
            spread(i - 2, owns[-1:])
        got = sibling(send)
        near = [(far[step - 1] + got[step].astype(F32)).astype(BF16) for step in range(1, outer)]
        gots.append(got)
        sums.append(near)
        crossed.append([across(value, step + 1) for step, value in enumerate(near)])
        return x, loaded

    def middle(i, hidden, after):
        start, count = chunks[i]
        at = slice(start * block, (start + count) * block)
        hidden, mine = middle_part(
            outer, at, owns[i], gots[i], crossed[i], hidden_grad, hidden, after
        )
        pieces.append([mine])
        if i != 1 or number < 4:
            spread(i, [])
        return hidden

    def spread(i, after):
        mine = in_order(pieces[i][0], after) if after else pieces[i][0]
        pieces[i] += [across(mine, step) for step in range(1, outer)]

    def relay(i, after):
        groups.append(pieces[i] + [sibling(packed(pieces[i], after))])

    def take_input(i, x, acc, after):
        weights = held[i] if i in held else [in_hbm(value) for value in both]
        write = (flipped[0] if i else None, state, full) if i < number - 2 else None
        ahead = (chunks[2], both) if i == 0 and number > 2 else None
        xt, total, whole, written, fetched = input_part(
            quarters, block, chunks[i], weights, i in held, groups[i], acc, number - 1 - i, x,
            after, write, ahead,
        )
        if i == 0:
            flipped.append(xt)
            totals.append(total)
        if written:
            state[:] = written
        if fetched:
            held[2] = fetched
        grads.append(whole)
        return total

    totals, state = [], []
    x, early, hidden, acc = inputs, [], None, None
    for i in range(number):
        x, early = forward(i, x, early)
        if i < 3:
            hidden = middle(i, hidden, [])
    for i in range(number):
        if i == 1:
            for j in range(len(pieces), number):
                hidden = middle(j, hidden, grads[-1:])
        relay(i, grads[1:2] + pieces[-1][1:2] if i > 1 else grads[:1] + crossed[-1][:1] if i else owns[-1:])
        acc = take_input(i, x, acc, sums[-1][:1] if i == 0 else pieces[-1][:1] if i == 1 else [])
    bits = columns.bit_length() - 1
    order = list(range(bits))
    orders = [order[:1] + order[2:] + order[1:2], order[1::-1] + order[2:]]
    stages = [acc] + token_sums(acc, columns, orders)
    input_grad = jnp.concatenate([half.astype(BF16) for half in stages[-1]], axis=1)
    for i in range(max(number - 2, 0), number):
        after = stages[min(i - max(number - 2, 0), bits)]
        state = weight_part(block, chunks[i], full, flipped[0], grads[i], state, after)
    return hidden, input_grad, state[0], state[1]


def solution(mesh):
    return jax.shard_map(
        functools.partial(local, mesh.shape["row"], mesh.shape["col"]),
        mesh=mesh,
        in_specs=(P(None, "row"), P("row", "col"), P("row", "col"), P("row", "col")),
        out_specs=(P("row", "col"), P("col", "row"), P("row", "col"), P("row", "col")),
        check_vma=False,
    )
```

```python
import functools
import math

import jax
import jax.numpy as jnp
from jax import lax
from jax.experimental import pallas as pl
from jax.experimental.pallas import tpu as pltpu
from jax.sharding import PartitionSpec as P

BF16 = jnp.bfloat16
F32 = jnp.float32
VMEM_BYTES = 6 * 1024 * 1024
SHARES = (2, 4, 5, 3)
SLOTS = 3
COST = 40
WHOLE = pl.BlockSpec(memory_space=pltpu.VMEM)
REMOTE = pl.BlockSpec(memory_space=pl.ANY)


def chunk_list(width):
    block = 256 if width % 256 == 0 else 128
    units = width // block
    total = sum(SHARES)
    edges = [0]
    run = 0
    for share in SHARES:
        run += share
        edges.append(max(min(units, round(units * run / total)), edges[-1]))
    return block, [(a, b - a) for a, b in zip(edges, edges[1:]) if b > a]


def call(kernel, name, in_specs, out_specs, out_shape, scratch, size, args, aliases=None, room=0):
    held = [item for item in scratch if len(getattr(item, 'shape', ())) > 2]
    room += VMEM_BYTES + sum(math.prod(item.shape) * item.dtype.itemsize for item in held)
    return pl.pallas_call(
        kernel,
        in_specs=in_specs,
        out_specs=out_specs,
        out_shape=out_shape,
        scratch_shapes=scratch,
        input_output_aliases=aliases or {},
        compiler_params=pltpu.CompilerParams(vmem_limit_bytes=room),
        cost_estimate=pl.CostEstimate(
            flops=COST * size, bytes_accessed=size, transcendentals=0
        ),
        name=name,
    )(*args)


def in_hbm(value):
    return pltpu.with_memory_space_constraint(value, pltpu.HBM)


def in_order(value, after):
    return call(
        lambda *refs: None,
        "in_order",
        [REMOTE] * (1 + len(after)),
        REMOTE,
        jax.ShapeDtypeStruct(value.shape, value.dtype),
        [],
        1,
        [value, *after],
        {0: 0},
    )


def pack_kernel(count, *refs):
    for step, ref in enumerate(refs[:count]):
        refs[-1][step] = ref[...]


def packed(values, after):
    return call(
        functools.partial(pack_kernel, len(values)),
        "packed",
        [WHOLE] * len(values) + [REMOTE] * len(after),
        WHOLE,
        jax.ShapeDtypeStruct((len(values), *values[0].shape), values[0].dtype),
        [],
        1,
        [*values, *after],
    )


def forward_kernel(layout, ins, outs, *refs):
    quarters, rows, block, start, count, following, first = layout
    given, made = refs[:ins], refs[ins : ins + outs]
    weights, total, sems, x_sem = refs[ins + outs :]
    sources = given[1:3]
    own_ref, far_ref, send_ref, *made = made
    x_ref, early = given[0], given[3:5]
    if first:
        x_copy = pltpu.make_async_copy(x_ref, made[0], x_sem)
        x_copy.start()
        x_ref, made = made[0], made[1:]
    slots = weights.shape[1]
    queue = [
        [
            pltpu.make_async_copy(
                source.at[:, pl.ds((start + j) * block, block)],
                weights.at[k, j % slots],
                sems.at[k, j % slots],
            )
            for k, source in enumerate(sources)
        ]
        for j in range(0 if first else 1, count)
    ]
    if made:
        queue.append(
            [
                pltpu.make_async_copy(
                    source.at[:, pl.ds(following * block, block)], target, sems.at[k, slots]
                )
                for k, (source, target) in enumerate(zip(sources, made))
            ]
        )
    for pair in queue[: slots - 1]:
        for copy in pair:
            copy.start()
    if first:
        x_copy.wait()
    outer = quarters // 2
    me = lax.axis_index("row")
    place, core = me // 2, me % 2
    x = x_ref[...]
    taken = 0
    for j in range(count):
        at = slice(j * block, (j + 1) * block)
        if first or j:
            for copy in queue[taken]:
                copy.wait()
            taken += 1
            more = taken + slots - 2
            for copy in queue[more] if more < len(queue) else []:
                copy.start()
            blocks = [weights[k, j % slots] for k in range(2)]
        else:
            blocks = [ref[...] for ref in early]
        for k in range(2):
            total[k] = jnp.dot(x, blocks[k], preferred_element_type=F32)
        for step in range(outer):
            there = (place + step) % outer * 2
            mine = pl.multiple_of((there + core) * rows, rows)
            other = pl.multiple_of((there + 1 - core) * rows, rows)
            for k in range(2):
                kept = total[k, pl.ds(mine, rows), :]
                if step == 0:
                    own_ref[k, :, at] = kept
                else:
                    far_ref[step - 1, k, :, at] = kept
                send_ref[step, k, :, at] = total[k, pl.ds(other, rows), :].astype(BF16)
    for pair in queue[taken:]:
        for copy in pair:
            copy.wait()


def forward_part(quarters, block, chunk, following, x, gate_weight, up_weight, early, after):
    tokens, depth = x.shape
    rows = tokens // quarters
    outer = quarters // 2
    start, count = chunk
    width = count * block
    first = not early
    out_shape = [
        jax.ShapeDtypeStruct((2, rows, width), F32),
        jax.ShapeDtypeStruct((outer - 1, 2, rows, width), F32),
        jax.ShapeDtypeStruct((outer, 2, rows, width), BF16),
    ]
    if first:
        x = in_hbm(x)
        out_shape.append(jax.ShapeDtypeStruct(x.shape, BF16))
    if following is not None:
        out_shape += [jax.ShapeDtypeStruct((depth, block), BF16)] * 2
    args = (x, in_hbm(gate_weight), in_hbm(up_weight), *early, *after)
    layout = (quarters, rows, block, start, count, following, first)
    return call(
        functools.partial(forward_kernel, layout, len(args), len(out_shape)),
        "forward_part",
        [REMOTE if first else WHOLE, REMOTE, REMOTE]
        + [WHOLE] * len(early)
        + [REMOTE] * len(after),
        [WHOLE] * len(out_shape),
        out_shape,
        [
            pltpu.VMEM((2, SLOTS, depth, block), BF16),
            pltpu.VMEM((2, tokens, block), F32),
            pltpu.SemaphoreType.DMA((2, SLOTS + 1)),
            pltpu.SemaphoreType.DMA,
        ],
        tokens * depth * width,
        args,
    )


def middle_kernel(outer, at, first, skipped, own_ref, got_ref, upstream_ref, *refs):
    far_refs, rest = refs[: outer - 1], refs[outer - 1 + skipped :]
    if not first:
        rest[1][...] = rest[0][...]
        rest = rest[1:]
    hidden_ref, grads_ref = rest
    gate_pre = own_ref[0] + got_ref[0, 0].astype(F32)
    up_pre = own_ref[1] + got_ref[0, 1].astype(F32)
    for far in far_refs:
        gate_pre += far[0].astype(F32)
        up_pre += far[1].astype(F32)
    sigma_gate = jax.nn.sigmoid(gate_pre)
    upstream = upstream_ref[:, at].astype(F32)
    gated = gate_pre * sigma_gate
    hidden_ref[:, at] = (gated * up_pre).astype(BF16)
    slope = sigma_gate * (1.0 + gate_pre * (1.0 - sigma_gate))
    grads_ref[0] = (upstream * up_pre * slope).astype(BF16)
    grads_ref[1] = (upstream * gated).astype(BF16)


def middle_part(outer, at, own, got, far, hidden_grad, hidden, after):
    rows, width = own.shape[1:]
    first = hidden is None
    args = [own, got, hidden_grad, *far, *after] + ([] if first else [hidden])
    return call(
        functools.partial(middle_kernel, outer, at, first, len(after)),
        "middle_part",
        [WHOLE] * (2 + outer) + [REMOTE] * len(after) + [WHOLE] * (not first),
        [WHOLE] * 2,
        [
            jax.ShapeDtypeStruct(hidden_grad.shape, BF16),
            jax.ShapeDtypeStruct((2, rows, width), BF16),
        ],
        [],
        rows * width,
        args,
    )


def input_kernel(layout, ins, outs, *refs):
    quarters, rows, block, chunk, held, first, last, skipped, write, old, ahead = layout
    given, made, scratch = refs[:ins], list(refs[ins : ins + outs]), list(refs[ins + outs :])
    (gate_ref, up_ref), given = given[:2], given[2 + skipped :]
    outer = quarters // 2
    pieces, given = given[: outer + 1], list(given[outer + 1 :])
    sources = (gate_ref, up_ref)
    depth = gate_ref.shape[0]
    half = depth // 2
    earlier = []
    if first:
        x_ref, xt_ref = given.pop(0), made.pop(0)
    else:
        earlier = [given.pop(0) for _ in range(old)]
    if write and not first:
        xt_ref = given.pop(0)
    if ahead and held:
        sources = (given.pop(0), given.pop(0))
    loaded = [made.pop() for _ in range(2)][::-1] if ahead else []
    grad_outs = [made.pop() for _ in range(2)][::-1] if write else []
    grads = made.pop()
    sums = made

    def fetch(columns, targets, sems):
        return [
            pltpu.make_async_copy(
                source.at[pl.ds(h * half, half), columns],
                target.at[pl.ds(h * half, half)],
                sems.at[k, h],
            )
            for h in range(2)
            for k, (source, target) in enumerate(zip(sources, targets))
        ]

    weights, copies, later, writes = (gate_ref, up_ref), [], [], []
    start, count = chunk
    if not held:
        store, sems = scratch.pop(0), scratch.pop(0)
        weights = (store.at[0], store.at[1])
        copies = fetch(pl.ds(start * block, count * block), weights, sems)
        for copy in copies:
            copy.start()
    if ahead:
        later = fetch(pl.ds(ahead[0] * block, ahead[1] * block), loaded, scratch.pop())
    if held:
        for copy in later:
            copy.start()
    me = lax.axis_index("row")
    place, core = me // 2, me % 2
    for step in range(outer):
        there = (place + outer - step) % outer * 2
        mine = pl.multiple_of((there + core) * rows, rows)
        other = pl.multiple_of((there + 1 - core) * rows, rows)
        for k in range(2):
            grads[k, pl.ds(mine, rows), :] = pieces[step][k]
            grads[k, pl.ds(other, rows), :] = pieces[outer][step, k]
    if first:
        xt_ref[...] = x_ref[...].T
    if write:
        products, sems = scratch
        writes = weight_terms(block, chunk, xt_ref, grads, grad_outs, products, sems)
    dims = (((1,), (1,)), ((), ()))
    flipped = [] if last else [grads[k].T for k in range(2)]
    deep = 256 if depth % 512 == 0 else 128
    for d in range(depth // deep):
        at = slice(d * deep, (d + 1) * deep)
        index, across = d * deep // half, slice(d * deep % half, d * deep % half + deep)
        if copies and d * deep % half == 0:
            copies[2 * index].wait()
            copies[2 * index + 1].wait()
            for copy in later[2 * index : 2 * index + 2]:
                copy.start()
        term = None
        if earlier:
            term = earlier[index][:, across] if last else earlier[0][at, :]
        for k in range(2):
            piece = weights[k][at, :]
            if last:
                product = lax.dot_general(grads[k], piece, dims, preferred_element_type=F32)
            else:
                product = jnp.dot(piece, flipped[k], preferred_element_type=F32)
            term = product if term is None else term + product
        if last:
            sums[index][:, across] = term
        elif len(sums) == 1:
            sums[0][at, :] = term
        else:
            sums[index][:, across] = term.T
    for copy in writes + later:
        copy.wait()


def input_part(quarters, block, chunk, weights, held, pieces, acc, final, x, after, write, ahead):
    depth, tokens = x.shape[1], x.shape[0]
    rows = tokens // quarters
    start, count = chunk
    width = count * block
    first, last = acc is None, final == 0
    args = [*weights, *after, *pieces, *([x] if first else acc)]
    in_specs = [WHOLE if held else REMOTE] * 2 + [REMOTE] * len(after)
    in_specs += [WHOLE] * (len(args) - len(in_specs))
    out_shape = [jax.ShapeDtypeStruct((depth, tokens), BF16)] if first else []
    out_shape += [jax.ShapeDtypeStruct((tokens, depth // 2), F32)] * 2 if final <= 1 else [
        jax.ShapeDtypeStruct((depth, tokens), F32)
    ]
    out_shape.append(jax.ShapeDtypeStruct((2, tokens, width), BF16))
    scratch, aliases, room = [], {}, 0
    if not held:
        scratch += [pltpu.VMEM((2, depth, width), BF16), pltpu.SemaphoreType.DMA((2, 2))]
    out_specs = [WHOLE] * len(out_shape)
    if write:
        xt, state, full = write
        args += [] if first else [xt]
        in_specs += [] if first else [WHOLE]
    if ahead:
        (chunk_ahead, sources), ahead = ahead, ahead[0]
        if held:
            args += [in_hbm(value) for value in sources]
            in_specs += [REMOTE] * 2
    if write:
        aliases = {len(args) + k: len(out_shape) + k for k in range(len(state))}
        args += [in_hbm(value) for value in state]
        in_specs += [REMOTE] * len(state)
        out_shape += [pltpu.HBM((depth, full), BF16)] * 2
        out_specs += [REMOTE] * 2
        scratch += [pltpu.VMEM((2, count, depth, block), BF16), pltpu.SemaphoreType.DMA((2, count))]
    if ahead:
        out_shape += [jax.ShapeDtypeStruct((depth, ahead[1] * block), BF16)] * 2
        out_specs += [WHOLE] * 2
        scratch.append(pltpu.SemaphoreType.DMA((2, 2)))
    if held or ahead:
        room = 4 * depth * max(width, ahead[1] * block if ahead else 0)
    old = 0 if first else len(acc)
    layout = (quarters, rows, block, chunk, held, first, last, len(after), bool(write), old, ahead)
    out = call(
        functools.partial(input_kernel, layout, len(args), len(out_shape)),
        "input_part",
        in_specs,
        out_specs,
        out_shape,
        scratch,
        tokens * depth * (1 if first else width),
        args,
        aliases,
        room,
    )
    out = list(out)
    xt = out.pop(0) if first else None
    fetched = [out.pop() for _ in range(2)][::-1] if ahead else None
    state = [out.pop() for _ in range(2)][::-1] if write else None
    return xt, out[:-1], out[-1], state, fetched


def weight_terms(block, chunk, xt_ref, grads_ref, outs, products, sems):
    start, count = chunk
    xt = xt_ref[...]
    copies = []
    for j in range(count):
        for k, out in enumerate(outs):
            piece = grads_ref[k, :, j * block : (j + 1) * block]
            products[k, j] = jnp.dot(xt, piece, preferred_element_type=F32).astype(BF16)
            copy = pltpu.make_async_copy(
                products.at[k, j], out.at[:, pl.ds((start + j) * block, block)], sems.at[k, j]
            )
            copy.start()
            copies.append(copy)
    return copies


def weight_kernel(block, chunk, skipped, xt_ref, grads_ref, *refs):
    *outs, products, sems = refs[skipped:]
    for copy in weight_terms(block, chunk, xt_ref, grads_ref, outs, products, sems):
        copy.wait()


def weight_part(block, chunk, full, xt, grads, state, after):
    depth, tokens = xt.shape
    count = chunk[1]
    args = [xt, grads, *after, *[in_hbm(value) for value in state]]
    first = len(args) - len(state)
    return call(
        functools.partial(weight_kernel, block, chunk, len(args) - 2),
        "weight_part",
        [WHOLE] * 2 + [REMOTE] * (len(args) - 2),
        [REMOTE] * 2,
        [pltpu.HBM((depth, full), BF16)] * 2,
        [pltpu.VMEM((2, count, depth, block), BF16), pltpu.SemaphoreType.DMA((2, count))],
        tokens * depth * count * block,
        args,
        {first + k: k for k in range(len(state))},
    )


def token_sums(halves, columns, orders):
    position = lax.axis_index("col")
    bits = len(orders[0])
    rows = halves[0].shape[0] // columns
    halves = [half.reshape((2,) * bits + (rows, half.shape[1])) for half in halves]
    lefts = [list(reversed(range(bits))) for _ in halves]
    stages = []
    for stage in range(bits):
        kept, got = [], []
        for half, left, order in zip(halves, lefts, orders):
            bit = order[stage]
            axis = left.index(bit)
            left.remove(bit)
            mine = (position // 2**bit) % 2
            send = lax.dynamic_index_in_dim(half, 1 - mine, axis, keepdims=False)
            moves = [(c, c ^ 2**bit) for c in range(columns)]
            got.append(lax.ppermute(send.astype(BF16), "col", moves))
            kept.append(lax.dynamic_index_in_dim(half, mine, axis, keepdims=False))
        halves = [keep + far.astype(F32) for keep, far in zip(kept, got)]
        stages.append(halves)
    return stages


def local(quarters, columns, inputs, gate_weight, up_weight, hidden_grad):
    outer = quarters // 2
    full = gate_weight.shape[1]
    block, chunks = chunk_list(full)
    swap = [(r, r ^ 1) for r in range(quarters)]

    def sibling(value):
        return lax.ppermute(value, "row", swap)

    def across(value, step):
        moves = [(r, (r // 2 + step) % outer * 2 + r % 2) for r in range(quarters)]
        return lax.ppermute(value, "row", moves)

    number = len(chunks)
    both = [gate_weight, up_weight]
    owns, gots, sums, crossed, pieces, groups, grads = [], [], [], [], [], [], []
    held, flipped = {}, []

    def forward(i, x, early):
        following = chunks[i + 1][0] if i + 1 < number else None
        after = sums[i - 1][:1] if i else []
        own, far, send, *loaded = forward_part(
            quarters, block, chunks[i], following, x, gate_weight, up_weight, early, after
        )
        owns.append(own)
        if i == 0:
            x, loaded = loaded[0], loaded[1:]
        elif i < 3:
            send = in_order(send, crossed[i - 1][:1] + pieces[i - 1][:1])
        else:
            if i == number - 1:
                relay(0, sums[-1][:1])
                take_input(0, x, None, [])
            send = in_order(send, crossed[i - 1][:1] + pieces[i - 1][:1] + pieces[i - 2][1:2] + grads)
        got = sibling(send)
        near = [(far[step - 1] + got[step].astype(F32)).astype(BF16) for step in range(1, outer)]
        gots.append(got)
        sums.append(near)
        crossed.append([across(value, step + 1) for step, value in enumerate(near)])
        return x, loaded

    def middle(i, hidden, after):
        start, count = chunks[i]
        at = slice(start * block, (start + count) * block)
        hidden, mine = middle_part(
            outer, at, owns[i], gots[i], crossed[i], hidden_grad, hidden, after
        )
        pieces.append([mine] + [across(mine, step) for step in range(1, outer)])
        return hidden

    def relay(i, after):
        groups.append(pieces[i] + [sibling(packed(pieces[i], after))])

    def take_input(i, x, acc, after):
        weights = held[i] if i in held else [in_hbm(value) for value in both]
        write = (flipped[0] if i else None, state, full) if i < number - 2 else None
        ahead = (chunks[2], both) if i == 0 and number > 2 else None
        xt, total, whole, written, fetched = input_part(
            quarters, block, chunks[i], weights, i in held, groups[i], acc, number - 1 - i, x,
            after, write, ahead,
        )
        if i == 0:
            flipped.append(xt)
            totals.append(total)
        if written:
            state[:] = written
        if fetched:
            held[2] = fetched
        grads.append(whole)
        return total

    totals, state = [], []
    x, early, hidden = inputs, [], None
    for i in range(number):
        x, early = forward(i, x, early)
        if i < 3:
            hidden = middle(i, hidden, pieces[0][1:2] if i == 2 else [])
    acc = None
    for i in range(number):
        if i == 0 and grads:
            acc = totals[0]
            continue
        after = sums[-1][:1] + pieces[i + 1][:1] if i == 1 and number > 3 else []
        relay(i, grads[1:2] + pieces[-1][:1] if i > 1 else sums[-1][:1])
        acc = take_input(i, x, acc, after)
        for j in range(len(pieces), number if i else 0):
            hidden = middle(j, hidden, grads[-1:])
    bits = columns.bit_length() - 1
    order = list(range(bits))
    orders = [order[:1] + order[2:] + order[1:2], order[1::-1] + order[2:]]
    stages = [acc] + token_sums(acc, columns, orders)
    input_grad = jnp.concatenate([half.astype(BF16) for half in stages[-1]], axis=1)
    for i in range(max(number - 2, 0), number):
        after = stages[min(i - max(number - 2, 0), bits)]
        state = weight_part(block, chunks[i], full, flipped[0], grads[i], state, after)
    return hidden, input_grad, state[0], state[1]


def solution(mesh):
    return jax.shard_map(
        functools.partial(local, mesh.shape["row"], mesh.shape["col"]),
        mesh=mesh,
        in_specs=(P(None, "row"), P("row", "col"), P("row", "col"), P("row", "col")),
        out_specs=(P("row", "col"), P("col", "row"), P("row", "col"), P("row", "col")),
        check_vma=False,
    )
```
